256 devices in a mesh: acq: 16 (over y, x), rows: 16 (over z, core).
Axes of the slice: x: 4, y: 4, z: 8, core: 2. Of those that a mesh axis runs over, the one named last changes fastest.
Arguments:
- slc: float32 [16, 2, 512, 4096], P('acq', None, 'rows'), may hold values from -6 to 6
- pair_index: int32 [16, 2], P('acq'), may hold values from 0 to 15, as said below
Outputs:
- products: float32 [16, 3, 512, 4096], P('acq', None, 'rows')
The draws below stay inside these ranges and needn't reach their ends.
Inputs may be any that keep to these rules, and one draw needn't show every extreme that they name: `pair_index`: pair p has reference acquisition p mod 16 and a secondary acquisition different from it.
All inputs are finite; a program needn't handle non-finite values.
Results may differ from the reference program's by a relative error of at most 0.00009.
Values sent between devices are 32-bit elements; how exact they have to be, the bound alone decides.
No kernel may reach another device: no remote copies, remote signals or barrier semaphores. Data moves between devices by JAX's collectives and lax.ppermute only.
A program may use at most 64 MiB of HBM per device.

```python
import jax
import jax.numpy as jnp
from jax import lax

COLS = 4096
LOOK_R = 5
LOOK_C = 19
PATCH = 32
ACQ = 16
PAIRS = 16
ROWS = 512


def draw_pair_index(key, part):
    key = jax.random.fold_in(key, 1)
    first = jnp.arange(PAIRS, dtype=jnp.int32) % ACQ
    offset = jax.random.randint(key, (PAIRS,), 1, ACQ, dtype=jnp.int32)
    second = (first + offset) % ACQ
    return jnp.stack([first, second], axis=1).astype(jnp.int32)


def shard_levels(key, extent, cuts, low, top_value):
    level = 1.0
    for axis_at, shards_of in cuts:
        steps = jax.random.uniform(jax.random.fold_in(jax.random.fold_in(key, 6), axis_at), (shards_of,), jnp.float32, low / len(cuts), top_value / len(cuts))
        level = level * jnp.repeat(jnp.exp(steps), extent[axis_at] // shards_of).reshape((-1,) + (1,) * (len(extent) - 1 - axis_at))
    return level


def noise(own_key, shape, spread, reach, pieces=(), held_as=jnp.bfloat16):
    values = jax.random.normal(own_key, shape, jnp.float32) * spread
    if len(pieces) > 0:
        values = shard_levels(own_key, shape, pieces, -0.22, 0.18) * values
    return jnp.clip(values, min=-reach, max=reach).astype(held_as)


def setup_inputs(seed: int = 0) -> dict:
    arg_keys = jax.random.split(jax.random.key(seed), 3)
    slc = noise(arg_keys[0], (ACQ, 2, ROWS, COLS), 1.0, 6.0, ((0, 16), (2, 16)), jnp.float32)
    pair_index = draw_pair_index(jax.random.fold_in(arg_keys[2], 71), 0)
    return dict(slc=slc, pair_index=pair_index)


def boxsum(field, rows_out, cols_out):
    total = field[..., 0:rows_out, :]
    for shift in range(1, LOOK_R):
        total = total + field[..., shift:shift + rows_out, :]
    result = total[..., :, 0:cols_out]
    for shift in range(1, LOOK_C):
        result = result + total[..., :, shift:shift + cols_out]
    return result

def goldstein(real_part, imag_part):
    height, width = real_part.shape
    patched = (real_part + 1j * imag_part).reshape(height // PATCH, PATCH, width // PATCH, PATCH)
    spectrum = jnp.fft.fft2(patched, axes=(1, 3))
    weight = jnp.sqrt(jnp.sqrt(jnp.real(spectrum) ** 2 + jnp.imag(spectrum) ** 2 + 1e-06))
    weight = weight / lax.optimization_barrier(jnp.mean(weight, axis=(1, 3), keepdims=True))
    filtered = jnp.fft.ifft2(spectrum * weight, axes=(1, 3))
    return (jnp.real(filtered).reshape(height, width), jnp.imag(filtered).reshape(height, width))

def pair_terms(first, second):
    rows_out = first.shape[1] - (LOOK_R - 1)
    cols_out = first.shape[2] - (LOOK_C - 1)
    cross_re = first[0] * second[0] + first[1] * second[1]
    cross_im = first[1] * second[0] - first[0] * second[1]
    power_a = first[0] * first[0] + first[1] * first[1]
    power_b = second[0] * second[0] + second[1] * second[1]
    sums = boxsum(jnp.stack([cross_re, cross_im, power_a, power_b]), rows_out, cols_out)
    scale = lax.rsqrt(sums[2] * sums[3] + 1e-06)
    gamma_re = sums[0] * scale
    gamma_im = sums[1] * scale
    coherence = jnp.sqrt(gamma_re * gamma_re + gamma_im * gamma_im)
    filt_re, filt_im = goldstein(gamma_re, gamma_im)
    return jnp.stack([coherence, filt_re, filt_im])

def reference(slc, pair_index):
    half_r = (LOOK_R - 1) // 2
    half_c = (LOOK_C - 1) // 2
    padded = jnp.pad(slc, ((0, 0), (0, 0), (half_r, half_r), (half_c, half_c)))

    def single(pair):
        return pair_terms(padded[pair[0]], padded[pair[1]])
    return lax.map(single, pair_index)
```

```python
import functools

import jax
import jax.numpy as jnp
import ml_dtypes
import numpy as np
from jax import lax
from jax.experimental import pallas as pl
from jax.experimental.pallas import tpu as pltpu
from jax.sharding import PartitionSpec as P

LOOK_R = 5
LOOK_C = 19
PATCH = 32
LANES = 128
BLOCK = 256
VMEM = pl.BlockSpec(memory_space=pltpu.VMEM)
SMEM = pl.BlockSpec(memory_space=pltpu.SMEM)
PARAMS = pltpu.CompilerParams(vmem_limit_bytes=40 * 1024 * 1024)
F32 = jnp.float32
BF16 = jnp.bfloat16


def cost(flops, moved):
    return pl.CostEstimate(flops=flops, bytes_accessed=moved, transcendentals=0)


def halves(matrix):
    high = matrix.astype(ml_dtypes.bfloat16)
    low = (matrix - high.astype(np.float64)).astype(ml_dtypes.bfloat16)
    return high, low


def split(x):
    high = x.astype(BF16)
    low = (x - high.astype(F32)).astype(BF16)
    return high, low


def constants():
    index = np.arange(PATCH)
    phase = 2.0 * np.pi / PATCH * (index[:, None] * index[None, :] % PATCH)
    c, s = np.cos(phase), np.sin(phase)
    eye = np.eye(LANES // PATCH)
    cb, sb = np.kron(eye, c), np.kron(eye, s)

    def three_rows(m):
        h, l = halves(m)
        return np.concatenate([h, h, l], axis=0)

    def three_cols(m):
        h, l = halves(m)
        return np.concatenate([h, h, l], axis=1)

    right = three_rows(np.block([[cb, -sb], [sb, cb]]))
    right_inv = three_rows(np.block([[cb, sb], [-sb, cb]]) / (PATCH * PATCH))
    left = three_cols(np.block([[c, s], [-s, c]]))
    left_inv = three_cols(np.block([[c, -s], [s, c]]))
    half = LOOK_C // 2
    row, col = np.arange(BLOCK)[:, None], np.arange(BLOCK)[None, :]
    near = (np.abs(row - LANES - col) <= half).astype(ml_dtypes.bfloat16)
    far = (np.abs(row + LANES - col) <= half).astype(ml_dtypes.bfloat16)
    band = np.concatenate([near, near, far, far], axis=0)
    mean = np.kron(np.eye(BLOCK // PATCH), np.full((PATCH, PATCH), 1.0 / (PATCH * PATCH))).astype(ml_dtypes.bfloat16)
    mean = np.concatenate([mean, mean], axis=0)
    return right, right_inv, left, left_inv, band, mean


def spread_chunks(slc, pair_index):
    count = slc.shape[3] // BLOCK

    def kernel(x_ref, pair_ref, o_ref):
        wanted = jnp.full((8, LANES), pair_ref[0, 1].astype(F32))
        for j in range(count):
            for k in range(2):
                cols = slice(BLOCK * j + LANES * k, BLOCK * j + LANES * (k + 1))
                for c in range(2):
                    o_ref[j, 64 * k + 32 * c : 64 * k + 32 * c + 32] = x_ref[0, c, :, cols]
            o_ref[j, 128:136] = wanted

    return pl.pallas_call(
        kernel,
        out_shape=jax.ShapeDtypeStruct((count, 136, LANES), F32),
        in_specs=[VMEM, SMEM],
        out_specs=VMEM,
        compiler_params=PARAMS,
        cost_estimate=cost(0, 2 << 20),
        name="spread_chunks",
    )(slc, pair_index)


def pick_chunks(held):
    count = held.shape[0]

    def kernel(v_ref, o_ref):
        for p in range(count):
            wanted = v_ref[p, 128:129, 0:1][0, 0].astype(jnp.int32)
            o_ref[p] = v_ref[wanted, 0:128]

    return pl.pallas_call(
        kernel,
        out_shape=jax.ShapeDtypeStruct((count, 128, LANES), F32),
        in_specs=[VMEM],
        out_specs=VMEM,
        compiler_params=PARAMS,
        cost_estimate=cost(0, 2 << 20),
        name="pick_chunks",
    )(held)


def edge_rows(slc, second, core):
    count = second.shape[0]

    def kernel(core_ref, a_ref, b_ref, near_ref, away_ref):
        even = core_ref[0] == 0
        for j in range(count):
            for k in range(2):
                cols = slice(BLOCK * j + LANES * k, BLOCK * j + LANES * (k + 1))
                for c in range(2):
                    at = slice(4 * c + 2 * k, 4 * c + 2 * k + 2)
                    base = 64 * k + 32 * c
                    for i, (top, low) in enumerate((
                        (a_ref[0, c, 0:2, cols], a_ref[0, c, 30:32, cols]),
                        (b_ref[j, base : base + 2], b_ref[j, base + 30 : base + 32]),
                    )):
                        near_ref[i, j, at] = jnp.where(even, low, top)
                        away_ref[i, j, at] = jnp.where(even, top, low)

    shape = jax.ShapeDtypeStruct((2, count, 8, LANES), F32)
    return pl.pallas_call(
        kernel,
        out_shape=(shape, shape),
        in_specs=[SMEM, VMEM, VMEM],
        out_specs=(VMEM, VMEM),
        compiler_params=PARAMS,
        cost_estimate=cost(0, 2 << 20),
        name="edge_rows",
    )(core, slc, second)


def own_sums(slc, second, band):
    count = second.shape[0]

    def kernel(a_ref, b_ref, w_ref, o_ref, rows_ref, high_ref, low_ref):
        zero8 = jnp.zeros((8, LANES), F32)
        for slot in range(8):
            rows_ref[slot, 0:8] = zero8
            rows_ref[slot, 40:48] = zero8
        zero = jnp.zeros((128, LANES), BF16)
        for ref in (high_ref, low_ref):
            ref[0, :, 0:LANES] = zero
            ref[count, :, LANES:BLOCK] = zero
        for t in range(2 * count):
            j, k = t // 2, t % 2
            cols = slice(LANES * t, LANES * (t + 1))
            a0, a1 = a_ref[0, 0, :, cols], a_ref[0, 1, :, cols]
            b0, b1 = b_ref[j, 64 * k : 64 * k + 32], b_ref[j, 64 * k + 32 : 64 * k + 64]
            fields = (a0 * b0 + a1 * b1, a1 * b0 - a0 * b1, a0 * a0 + a1 * a1, b0 * b0 + b1 * b1)
            at, side = (t + 1) // 2, (t + 1) % 2
            lanes = slice(LANES * side, LANES * (side + 1))
            for f, field in enumerate(fields):
                slot = 4 * (t % 2) + f
                rows_ref[slot, 8:40] = field
                total = field
                for shift in (6, 7, 9, 10):
                    total = total + rows_ref[slot, shift : shift + 32]
                high, low = split(total)
                high_ref[at, 32 * f : 32 * f + 32, lanes] = high
                low_ref[at, 32 * f : 32 * f + 32, lanes] = low
        for j in range(count):
            left = jnp.concatenate([high_ref[j], low_ref[j], high_ref[j + 1], low_ref[j + 1]], axis=1)
            o_ref[j] = jnp.dot(left, w_ref[...], preferred_element_type=F32)

    return pl.pallas_call(
        kernel,
        out_shape=jax.ShapeDtypeStruct((count, 128, BLOCK), F32),
        in_specs=[VMEM, VMEM, VMEM],
        out_specs=VMEM,
        scratch_shapes=[
            pltpu.VMEM((8, 48, LANES), F32),
            pltpu.VMEM((count + 1, 128, BLOCK), BF16),
            pltpu.VMEM((count + 1, 128, BLOCK), BF16),
        ],
        compiler_params=PARAMS,
        cost_estimate=cost(4 << 30, 8 << 20),
        name="own_sums",
    )(slc, second, band)


def filtered(sums, near, away, core, right, right_inv, left, left_inv, band, mean):
    count = sums.shape[0]

    def kernel(core_ref, s_ref, near_ref, away_ref, r_ref, ri_ref, l_ref, li_ref, w_ref, m_ref, o_ref,
               edge_ref, gh_ref, gl_ref, y_ref, vh_ref, vl_ref, sum_ref):
        even = core_ref[0] == 0
        sub = lax.broadcasted_iota(jnp.int32, (8, LANES), 0)
        odd_row = sub % 2 == 1
        edge_ref[...] = jnp.zeros(edge_ref.shape, F32)
        for j in range(count):
            for place in range(2):
                if place == 0:
                    pick = lambda i: jnp.where(even, away_ref[i, j], near_ref[i, j])
                else:
                    pick = lambda i: jnp.where(even, near_ref[i, j], away_ref[i, j])
                a, b = pick(0), pick(1)
                turned = pltpu.roll(b, 4, 0)
                mixed = a * turned
                same, aa, bb = a * b, a * a, b * b
                fields = (
                    same + pltpu.roll(same, 4, 0),
                    pltpu.roll(mixed, 4, 0) - mixed,
                    aa + pltpu.roll(aa, 4, 0),
                    bb + pltpu.roll(bb, 4, 0),
                )
                for f, field in enumerate(fields):
                    if place == 0:
                        field = jnp.where(odd_row, field, field + pltpu.roll(field, 7, 0))
                    else:
                        field = jnp.where(odd_row, field + pltpu.roll(field, 1, 0), field)
                    row = 8 * f + 6 * place
                    edge_ref[j, row : row + 2, LANES:BLOCK] = field[0:2]
                    edge_ref[j + 1, row : row + 2, 0:LANES] = field[2:4]
        top_half = lax.broadcasted_iota(jnp.int32, (8, BLOCK), 0) < 4
        for j in range(count):
            h0, l0 = split(edge_ref[j])
            h1, l1 = split(edge_ref[j + 1])
            more = jnp.dot(jnp.concatenate([h0, l0, h1, l1], axis=1), w_ref[...], preferred_element_type=F32)
            total = []
            for f in range(4):
                extra = more[8 * f : 8 * f + 8]
                first = s_ref[j, 32 * f : 32 * f + 8] + jnp.where(top_half, extra, 0.0)
                last = s_ref[j, 32 * f + 24 : 32 * f + 32] + jnp.where(top_half, 0.0, extra)
                total.append(jnp.concatenate([first, s_ref[j, 32 * f + 8 : 32 * f + 24], last], axis=0))
            scale = lax.rsqrt(total[2] * total[3] + 1e-06)
            gr, gi = total[0] * scale, total[1] * scale
            o_ref[0, 0, :, BLOCK * j : BLOCK * (j + 1)] = jnp.sqrt(gr * gr + gi * gi)
            rh, rl = split(gr)
            ih, il = split(gi)
            for k in range(2):
                at, cols = slice(64 * j + 32 * k, 64 * j + 32 * k + 32), slice(LANES * k, LANES * (k + 1))
                gh_ref[at, 0:LANES] = rh[:, cols]
                gh_ref[at, LANES:BLOCK] = ih[:, cols]
                gl_ref[at, 0:LANES] = rl[:, cols]
                gl_ref[at, LANES:BLOCK] = il[:, cols]
        step = 256
        for m in range(0, 64 * count, step):
            h, l = gh_ref[m : m + step], gl_ref[m : m + step]
            y_ref[m : m + step] = jnp.dot(jnp.concatenate([h, l, h], axis=1), r_ref[...], preferred_element_type=F32)
        for j in range(count):
            one, two = slice(64 * j, 64 * j + 32), slice(64 * j + 32, 64 * j + 64)
            yr = jnp.concatenate([y_ref[one, 0:LANES], y_ref[two, 0:LANES]], axis=1)
            yi = jnp.concatenate([y_ref[one, LANES:BLOCK], y_ref[two, LANES:BLOCK]], axis=1)
            h, l = split(jnp.concatenate([yr, yi], axis=0))
            z = jnp.dot(l_ref[...], jnp.concatenate([h, l, h], axis=0), preferred_element_type=F32)
            zr, zi = z[0:32], z[32:64]
            weight = lax.rsqrt(lax.rsqrt(zr * zr + zi * zi + 1e-06))
            sum_ref[j : j + 1] = jnp.sum(weight, axis=0, keepdims=True)
            h, l = split(jnp.concatenate([zr * weight, zi * weight], axis=0))
            v = jnp.dot(li_ref[...], jnp.concatenate([h, l, h], axis=0), preferred_element_type=F32)
            h, l = split(v)
            for ref, part in ((vh_ref, h), (vl_ref, l)):
                ref[one, 0:LANES] = part[0:32, 0:LANES]
                ref[one, LANES:BLOCK] = part[32:64, 0:LANES]
                ref[two, 0:LANES] = part[0:32, LANES:BLOCK]
                ref[two, LANES:BLOCK] = part[32:64, LANES:BLOCK]
        h, l = split(sum_ref[...])
        inverse = 1.0 / jnp.dot(jnp.concatenate([h, l], axis=1), m_ref[...], preferred_element_type=F32)
        sum_ref[...] = inverse
        for m in range(0, 64 * count, step):
            h, l = vh_ref[m : m + step], vl_ref[m : m + step]
            out = jnp.dot(jnp.concatenate([h, l, h], axis=1), ri_ref[...], preferred_element_type=F32)
            for n in range(step // 32):
                t = m // 32 + n
                factor = sum_ref[t // 2 : t // 2 + 1, LANES * (t % 2) : LANES * (t % 2 + 1)]
                cols = slice(LANES * t, LANES * (t + 1))
                o_ref[0, 1, :, cols] = out[32 * n : 32 * n + 32, 0:LANES] * factor
                o_ref[0, 2, :, cols] = out[32 * n : 32 * n + 32, LANES:BLOCK] * factor

    return pl.pallas_call(
        kernel,
        out_shape=jax.ShapeDtypeStruct((1, 3, 32, BLOCK * count), F32),
        in_specs=[SMEM] + [VMEM] * 9,
        out_specs=VMEM,
        scratch_shapes=[
            pltpu.VMEM((count + 1, 32, BLOCK), F32),
            pltpu.VMEM((64 * count, BLOCK), BF16),
            pltpu.VMEM((64 * count, BLOCK), BF16),
            pltpu.VMEM((64 * count, BLOCK), F32),
            pltpu.VMEM((64 * count, BLOCK), BF16),
            pltpu.VMEM((64 * count, BLOCK), BF16),
            pltpu.VMEM((count, BLOCK), F32),
        ],
        compiler_params=PARAMS,
        cost_estimate=cost(8 << 30, 8 << 20),
        name="filtered",
    )(core, sums, near, away, right, right_inv, left, left_inv, band, mean)


def on_device(slc, pair_index):
    right, right_inv, left, left_inv, band, mean = (jnp.asarray(m) for m in constants())
    blocks = lax.axis_size("rows")
    core = (lax.axis_index("rows") % 2).astype(jnp.int32).reshape(1)
    held = lax.all_to_all(spread_chunks(slc, pair_index), "acq", 0, 0)
    second = lax.all_to_all(pick_chunks(held), "acq", 0, 0)
    near, away = edge_rows(slc, second, core)
    away = lax.ppermute(away, "rows", [(i, i + 1) for i in range(1, blocks - 1, 2)] + [(i + 1, i) for i in range(1, blocks - 1, 2)])
    near = lax.ppermute(near, "rows", [(i, i ^ 1) for i in range(blocks)])
    sums = own_sums(slc, second, band)
    return filtered(sums, near, away, core, right, right_inv, left, left_inv, band, mean)


def solution(mesh):
    return jax.shard_map(
        on_device,
        mesh=mesh,
        in_specs=(P("acq", None, "rows", None), P("acq", None)),
        out_specs=P("acq", None, "rows", None),
        check_vma=False,
    )
```

```python
import functools

import jax
import jax.numpy as jnp
import ml_dtypes
import numpy as np
from jax import lax
from jax.experimental import pallas as pl
from jax.experimental.pallas import tpu as pltpu
from jax.sharding import PartitionSpec as P

LOOK_R = 5
LOOK_C = 19
PATCH = 32
LANES = 128
BLOCK = 256
OWN_GROUP = 16
LATE_GROUPS = 4
EARLY_GROUPS = 4
EDGE_GROUP = 8
VMEM = pl.BlockSpec(memory_space=pltpu.VMEM)
SMEM = pl.BlockSpec(memory_space=pltpu.SMEM)
PARAMS = pltpu.CompilerParams(vmem_limit_bytes=40 * 1024 * 1024)
F32 = jnp.float32
BF16 = jnp.bfloat16


def cost(flops, moved):
    return pl.CostEstimate(flops=flops, bytes_accessed=moved, transcendentals=0)


def halves(matrix):
    high = matrix.astype(ml_dtypes.bfloat16)
    low = (matrix - high.astype(np.float64)).astype(ml_dtypes.bfloat16)
    return high, low


def split(x):
    high = x.astype(BF16)
    low = (x - high.astype(F32)).astype(BF16)
    return high, low


def constants():
    index = np.arange(PATCH)
    phase = 2.0 * np.pi / PATCH * (index[:, None] * index[None, :] % PATCH)
    c, s = np.cos(phase), np.sin(phase)
    eye = np.eye(LANES // PATCH)
    cb, sb = np.kron(eye, c), np.kron(eye, s)

    def three_rows(m):
        h, l = halves(m)
        return np.concatenate([h, h, l], axis=0)

    def three_cols(m):
        h, l = halves(m)
        return np.concatenate([h, h, l], axis=1)

    right = three_rows(np.block([[cb, -sb], [sb, cb]]))
    right_inv = three_rows(np.block([[cb, sb], [-sb, cb]]) / (PATCH * PATCH))
    left = three_cols(np.block([[c, s], [-s, c]]))
    left_inv = three_cols(np.block([[c, -s], [s, c]]))
    half = LOOK_C // 2
    row, col = np.arange(BLOCK)[:, None], np.arange(BLOCK)[None, :]
    near = (np.abs(row - LANES - col) <= half).astype(ml_dtypes.bfloat16)
    far = (np.abs(row + LANES - col) <= half).astype(ml_dtypes.bfloat16)
    band = np.concatenate([near, near, far, far], axis=0)
    mean = np.kron(np.eye(BLOCK // PATCH), np.full((PATCH, PATCH), 1.0 / (PATCH * PATCH))).astype(ml_dtypes.bfloat16)
    mean = np.concatenate([mean, mean], axis=0)
    return right, right_inv, left, left_inv, band, mean


def spread_chunks(slc, pair_index, core):
    count = slc.shape[3] // BLOCK

    def kernel(core_ref, x_ref, pair_ref, o_ref, wanted_ref, held_ref, pair_sem, in_sem, out_sem):
        pair_copy = pltpu.make_async_copy(pair_ref, wanted_ref, pair_sem)
        pair_copy.start()

        def start(first, last, sem):
            for j in range(first, last):
                for k in range(2):
                    cols = slice(BLOCK * j + LANES * k, BLOCK * j + LANES * (k + 1))
                    for c in range(2):
                        rows = slice(64 * k + 32 * c, 64 * k + 32 * c + 32)
                        pltpu.make_async_copy(x_ref.at[0, c, :, cols], held_ref.at[j, rows], sem).start()

        def wait(first, last, sem):
            part = held_ref.at[first:last, 0:128]
            pltpu.make_async_copy(part, part, sem).wait()

        def out(first, last, sem):
            return pltpu.make_async_copy(held_ref.at[first:last], o_ref.at[first:last], sem)

        def fill():
            pair_copy.wait()
            wanted = jnp.full((8, LANES), wanted_ref[0, 1].astype(F32))
            for j in range(count):
                held_ref[j, 128:136] = wanted

        @pl.when(core_ref[0] == 0)
        def _():
            n = count // LATE_GROUPS
            for g in range(LATE_GROUPS):
                start(g * n, g * n + n, in_sem.at[g])
                if g == 0:
                    fill()
                wait(g * n, g * n + n, in_sem.at[g])
                copy = out(g * n, g * n + n, out_sem.at[g])
                copy.start()
                copy.wait()

        @pl.when(core_ref[0] != 0)
        def _():
            n = count // EARLY_GROUPS
            for g in range(EARLY_GROUPS):
                start(g * n, g * n + n, in_sem.at[g])
            fill()
            copies = [out(g * n, g * n + n, out_sem.at[g]) for g in range(EARLY_GROUPS)]
            for g in range(EARLY_GROUPS):
                wait(g * n, g * n + n, in_sem.at[g])
                copies[g].start()
            for copy in copies:
                copy.wait()

    hbm = pl.BlockSpec(memory_space=pltpu.HBM)
    return pl.pallas_call(
        kernel,
        out_shape=jax.ShapeDtypeStruct((count, 136, LANES), F32),
        in_specs=[SMEM, hbm, hbm],
        out_specs=hbm,
        scratch_shapes=[
            pltpu.SMEM((1, 2), jnp.int32),
            pltpu.VMEM((count, 136, LANES), F32),
            pltpu.SemaphoreType.DMA,
            pltpu.SemaphoreType.DMA((max(LATE_GROUPS, EARLY_GROUPS),)),
            pltpu.SemaphoreType.DMA((max(LATE_GROUPS, EARLY_GROUPS),)),
        ],
        compiler_params=pltpu.CompilerParams(vmem_limit_bytes=60 * 1024 * 1024),
        cost_estimate=cost(0, 2 << 20),
        name="spread_chunks",
    )(core, slc, pair_index)


def pick_chunks(held):
    count = held.shape[0]

    def kernel(v_ref, o_ref):
        for p in range(count):
            wanted = v_ref[p, 128:129, 0:1][0, 0].astype(jnp.int32)
            o_ref[p] = v_ref[wanted, 0:128]

    return pl.pallas_call(
        kernel,
        out_shape=jax.ShapeDtypeStruct((count, 128, LANES), F32),
        in_specs=[VMEM],
        out_specs=VMEM,
        compiler_params=PARAMS,
        cost_estimate=cost(0, 2 << 20),
        name="pick_chunks",
    )(held)


def first_sides(core, top, low):
    return jnp.where(core == 0, low, top), jnp.where(core == 0, top, low)


def edge_rows_first(slc, core):
    count = slc.shape[3] // BLOCK

    def kernel(core_ref, a_ref, near_ref, away_ref):
        for j in range(count):
            for k in range(2):
                cols = slice(BLOCK * j + LANES * k, BLOCK * j + LANES * (k + 1))
                for c in range(2):
                    at = slice(4 * c + 2 * k, 4 * c + 2 * k + 2)
                    near_ref[j, at], away_ref[j, at] = first_sides(
                        core_ref[0], a_ref[0, c, 0:2, cols], a_ref[0, c, 30:32, cols]
                    )

    shape = jax.ShapeDtypeStruct((count, 8, LANES), F32)
    return pl.pallas_call(
        kernel,
        out_shape=(shape, shape),
        in_specs=[SMEM, VMEM],
        out_specs=(VMEM, VMEM),
        compiler_params=PARAMS,
        cost_estimate=cost(0, 1 << 20),
        name="edge_rows_first",
    )(core, slc)


def edge_rows_second(second, core):
    count = second.shape[0]

    def kernel(core_ref, b_ref, near_ref, away_ref):
        for j in range(count):
            for k in range(2):
                for c in range(2):
                    at = slice(4 * c + 2 * k, 4 * c + 2 * k + 2)
                    base = 64 * k + 32 * c
                    near_ref[j, at], away_ref[j, at] = first_sides(
                        core_ref[0], b_ref[j, base : base + 2], b_ref[j, base + 30 : base + 32]
                    )

    shape = jax.ShapeDtypeStruct((count, 8, LANES), F32)
    return pl.pallas_call(
        kernel,
        out_shape=(shape, shape),
        in_specs=[SMEM, VMEM],
        out_specs=(VMEM, VMEM),
        compiler_params=PARAMS,
        cost_estimate=cost(0, 1 << 20),
        name="edge_rows_second",
    )(core, second)


def gamma_of(total):
    scale = lax.rsqrt(total[2] * total[3] + 1e-06)
    gr, gi = total[0] * scale, total[1] * scale
    return gr, gi, jnp.sqrt(gr * gr + gi * gi)


def put_tiles(ref, j, real, imag):
    for k in range(2):
        cols = slice(LANES * k, LANES * (k + 1))
        ref[2 * j + k, :, 0:LANES] = real[:, cols]
        ref[2 * j + k, :, LANES:BLOCK] = imag[:, cols]


def get_tiles(ref, j):
    real = jnp.concatenate([ref[2 * j, :, 0:LANES], ref[2 * j + 1, :, 0:LANES]], axis=1)
    imag = jnp.concatenate([ref[2 * j, :, LANES:BLOCK], ref[2 * j + 1, :, LANES:BLOCK]], axis=1)
    return jnp.concatenate([real, imag], axis=0)


def box_columns(high_ref, low_ref, band, start, n):
    rows = n * high_ref.shape[1]
    parts = [ref[start + d : start + d + n].reshape(rows, BLOCK) for d in range(2) for ref in (high_ref, low_ref)]
    return jnp.dot(jnp.concatenate(parts, axis=1), band, preferred_element_type=F32)


def staggered(count, group, stages):
    starts = list(range(0, count, group))
    for t in range(len(starts) + len(stages) - 1):
        for s in reversed(range(len(stages))):
            if 0 <= t - s < len(starts):
                stages[s](starts[t - s])


def own_part(slc, second, band, right):
    count = second.shape[0]
    group = OWN_GROUP

    def kernel(a_ref, b_ref, w_ref, r_ref, y_ref, edge_ref, coh_ref, rows_ref, high_ref, low_ref, gh_ref, gl_ref):
        zero8 = jnp.zeros((8, LANES), F32)
        for slot in range(8):
            rows_ref[slot, 0:8] = zero8
            rows_ref[slot, 40:48] = zero8
        zero = jnp.zeros((128, LANES), BF16)
        for ref in (high_ref, low_ref):
            ref[0, :, 0:LANES] = zero
            ref[count, :, LANES:BLOCK] = zero
        sub = lax.broadcasted_iota(jnp.int32, (8, BLOCK), 0)
        row = lax.broadcasted_iota(jnp.int32, (32, BLOCK), 0)
        inner = (row >= 2) & (row < 30)

        def row_sums(g):
            for t in range(2 * g + 1 if g else 0, min(2 * (g + group) + 1, 2 * count)):
                j, k = t // 2, t % 2
                cols = slice(LANES * t, LANES * (t + 1))
                a0, a1 = a_ref[0, 0, :, cols], a_ref[0, 1, :, cols]
                b0, b1 = b_ref[j, 64 * k : 64 * k + 32], b_ref[j, 64 * k + 32 : 64 * k + 64]
                fields = (a0 * b0 + a1 * b1, a1 * b0 - a0 * b1, a0 * a0 + a1 * a1, b0 * b0 + b1 * b1)
                at, side = (t + 1) // 2, (t + 1) % 2
                lanes = slice(LANES * side, LANES * (side + 1))
                for f, field in enumerate(fields):
                    slot = 4 * (t % 2) + f
                    rows_ref[slot, 8:40] = field
                    total = field
                    for shift in (6, 7, 9, 10):
                        total = total + rows_ref[slot, shift : shift + 32]
                    high, low = split(total)
                    high_ref[at, 32 * f : 32 * f + 32, lanes] = high
                    low_ref[at, 32 * f : 32 * f + 32, lanes] = low

        def gamma(g):
            sums = box_columns(high_ref, low_ref, w_ref[...], g, group)
            for j in range(g, g + group):
                total = [sums[128 * (j - g) + 32 * f : 128 * (j - g) + 32 * f + 32] for f in range(4)]
                for f in range(4):
                    edge_ref[j, 8 * f : 8 * f + 8] = jnp.where(sub < 4, total[f][0:8], total[f][24:32])
                gr, gi, coherence = gamma_of(total)
                coh_ref[:, BLOCK * j : BLOCK * (j + 1)] = coherence
                gr, gi = jnp.where(inner, gr, 0.0), jnp.where(inner, gi, 0.0)
                rh, rl = split(gr)
                ih, il = split(gi)
                put_tiles(gh_ref, j, rh, ih)
                put_tiles(gl_ref, j, rl, il)

        def transform(g):
            m, n = 2 * g, 2 * group
            h, l = (ref[m : m + n].reshape(32 * n, BLOCK) for ref in (gh_ref, gl_ref))
            y = jnp.dot(jnp.concatenate([h, l, h], axis=1), r_ref[...], preferred_element_type=F32)
            y_ref[m : m + n] = y.reshape(n, 32, BLOCK)

        staggered(count, group, (row_sums, gamma, transform))

    return pl.pallas_call(
        kernel,
        out_shape=(
            jax.ShapeDtypeStruct((2 * count, 32, BLOCK), F32),
            jax.ShapeDtypeStruct((count, 32, BLOCK), F32),
            jax.ShapeDtypeStruct((32, BLOCK * count), F32),
        ),
        in_specs=[VMEM] * 4,
        out_specs=(VMEM, VMEM, VMEM),
        scratch_shapes=[
            pltpu.VMEM((8, 48, LANES), F32),
            pltpu.VMEM((count + 1, 128, BLOCK), BF16),
            pltpu.VMEM((count + 1, 128, BLOCK), BF16),
            pltpu.VMEM((2 * count, 32, BLOCK), BF16),
            pltpu.VMEM((2 * count, 32, BLOCK), BF16),
        ],
        compiler_params=PARAMS,
        cost_estimate=cost(4 << 30, 12 << 20),
        name="own_part",
    )(slc, second, band, right)


def with_edges(half_spectrum, edge_sums, coherence, halos, core, right, right_inv, left, left_inv, band, mean):
    count = edge_sums.shape[0]
    group = EDGE_GROUP

    def kernel(core_ref, yin_ref, edge_ref, coh_ref, an_ref, aw_ref, bn_ref, bw_ref,
               r_ref, ri_ref, l_ref, li_ref, w_ref, m_ref, o_ref,
               part_ref, high_ref, low_ref, g_ref, y_ref, z_ref, vh_ref, vl_ref, strip_ref, out_ref, sem):
        copies = [pltpu.make_async_copy(coh_ref.at[8:24], o_ref.at[0, 0, 8:24], sem.at[0])]
        copies[0].start()
        even = core_ref[0] == 0
        odd_row = lax.broadcasted_iota(jnp.int32, (8, LANES), 0) % 2 == 1
        sub = lax.broadcasted_iota(jnp.int32, (8, BLOCK), 0)
        outer = (sub < 2) | (sub >= 6)
        part_ref[...] = jnp.zeros(part_ref.shape, F32)
        for j in range(count):
            for place in range(2):
                a, b = (
                    jnp.where(even == (place == 1), near[j], away[j])
                    for near, away in ((an_ref, aw_ref), (bn_ref, bw_ref))
                )
                mixed = a * pltpu.roll(b, 4, 0)
                same, aa, bb = a * b, a * a, b * b
                fields = (
                    same + pltpu.roll(same, 4, 0),
                    pltpu.roll(mixed, 4, 0) - mixed,
                    aa + pltpu.roll(aa, 4, 0),
                    bb + pltpu.roll(bb, 4, 0),
                )
                for f, field in enumerate(fields):
                    if place == 0:
                        field = jnp.where(odd_row, field, field + pltpu.roll(field, 7, 0))
                    else:
                        field = jnp.where(odd_row, field + pltpu.roll(field, 1, 0), field)
                    row = 8 * f + 6 * place
                    part_ref[j, row : row + 2, LANES:BLOCK] = field[0:2]
                    part_ref[j + 1, row : row + 2, 0:LANES] = field[2:4]
        for j in range(count + 1):
            high_ref[j], low_ref[j] = split(part_ref[j])

        def gamma(g):
            more = box_columns(high_ref, low_ref, w_ref[...], g, group)
            for j in range(g, g + group):
                at = 32 * (j - g)
                total = [edge_ref[j, 8 * f : 8 * f + 8] + more[at + 8 * f : at + 8 * f + 8] for f in range(4)]
                gr, gi, coherence = gamma_of(total)
                cols = slice(BLOCK * j, BLOCK * (j + 1))
                strip_ref[0, :, cols] = jnp.where(sub < 2, coherence, coh_ref[0:8, cols])
                strip_ref[1, :, cols] = jnp.where(sub >= 6, coherence, coh_ref[24:32, cols])
                put_tiles(g_ref, j, jnp.where(outer, gr, 0.0), jnp.where(outer, gi, 0.0))

        def transform(g):
            m, n = 2 * g, 2 * group
            h, l = split(g_ref[m : m + n].reshape(8 * n, BLOCK))
            y = jnp.dot(jnp.concatenate([h, l, h], axis=1), r_ref[...], preferred_element_type=F32)
            for t in range(n):
                more = y[8 * t : 8 * t + 8]
                y_ref[m + t, 0:8] = yin_ref[m + t, 0:8] + jnp.where(sub < 4, more, 0.0)
                y_ref[m + t, 8:24] = yin_ref[m + t, 8:24]
                y_ref[m + t, 24:32] = yin_ref[m + t, 24:32] + jnp.where(sub < 4, 0.0, more)

        def forward(g):
            for j in range(g, g + group):
                h, l = split(get_tiles(y_ref, j))
                z_ref[j] = jnp.dot(l_ref[...], jnp.concatenate([h, l, h], axis=0), preferred_element_type=F32)

        sums = {}

        def backward(g):
            parts = []
            for j in range(g, g + group):
                zr, zi = z_ref[j, 0:32], z_ref[j, 32:64]
                weight = lax.rsqrt(lax.rsqrt(zr * zr + zi * zi + 1e-06))
                parts.append(weight[0:8] + weight[8:16] + weight[16:24] + weight[24:32])
                h, l = split(jnp.concatenate([zr * weight, zi * weight], axis=0))
                v = jnp.dot(li_ref[...], jnp.concatenate([h, l, h], axis=0), preferred_element_type=F32)
                h, l = split(v)
                put_tiles(vh_ref, j, h[0:32], h[32:64])
                put_tiles(vl_ref, j, l[0:32], l[32:64])
            h, l = split(jnp.concatenate(parts, axis=0))
            total = jnp.dot(jnp.concatenate([h, l], axis=1), m_ref[...], preferred_element_type=F32)
            sums[g] = 1.0 / jnp.sum(total.reshape(group, 8, BLOCK), axis=1, keepdims=True)

        def finish(g):
            m, n = 2 * g, 2 * group
            h, l = (ref[m : m + n].reshape(32 * n, BLOCK) for ref in (vh_ref, vl_ref))
            out = jnp.dot(jnp.concatenate([h, l, h], axis=1), ri_ref[...], preferred_element_type=F32)
            for t in range(n):
                factor = sums[g][t // 2, :, LANES * (t % 2) : LANES * (t % 2 + 1)]
                cols = slice(LANES * (m + t), LANES * (m + t + 1))
                out_ref[0, :, cols] = out[32 * t : 32 * t + 32, 0:LANES] * factor
                out_ref[1, :, cols] = out[32 * t : 32 * t + 32, LANES:BLOCK] * factor
            cols = slice(LANES * m, LANES * (m + n))
            copy = pltpu.make_async_copy(out_ref.at[:, :, cols], o_ref.at[0, 1:3, :, cols], sem.at[3 + g // group])
            copy.start()
            copies.append(copy)
            if g + group == count:
                for i in range(2):
                    copy = pltpu.make_async_copy(strip_ref.at[i], o_ref.at[0, 0, 24 * i : 24 * i + 8], sem.at[1 + i])
                    copy.start()
                    copies.append(copy)

        staggered(count, group, (gamma, transform, forward, backward, finish))
        for copy in copies:
            copy.wait()

    return pl.pallas_call(
        kernel,
        out_shape=jax.ShapeDtypeStruct((1, 3, 32, BLOCK * count), F32),
        in_specs=[SMEM] + [VMEM] * 13,
        out_specs=pl.BlockSpec(memory_space=pltpu.HBM),
        scratch_shapes=[
            pltpu.VMEM((count + 1, 32, BLOCK), F32),
            pltpu.VMEM((count + 1, 32, BLOCK), BF16),
            pltpu.VMEM((count + 1, 32, BLOCK), BF16),
            pltpu.VMEM((2 * count, 8, BLOCK), F32),
            pltpu.VMEM((2 * count, 32, BLOCK), F32),
            pltpu.VMEM((count, 64, BLOCK), F32),
            pltpu.VMEM((2 * count, 32, BLOCK), BF16),
            pltpu.VMEM((2 * count, 32, BLOCK), BF16),
            pltpu.VMEM((2, 8, BLOCK * count), F32),
            pltpu.VMEM((2, 32, BLOCK * count), F32),
            pltpu.SemaphoreType.DMA((3 + count // group,)),
        ],
        compiler_params=PARAMS,
        cost_estimate=cost(8 << 30, 8 << 20),
        name="with_edges",
    )(core, half_spectrum, edge_sums, coherence, *halos, right, right_inv, left, left_inv, band, mean)


def on_device(slc, pair_index):
    right, right_inv, left, left_inv, band, mean = (jnp.asarray(m) for m in constants())
    blocks = lax.axis_size("rows")
    core = (lax.axis_index("rows") % 2).astype(jnp.int32).reshape(1)
    between = range(1, blocks - 1, 2)
    far = [(i, i + 1) for i in between] + [(i + 1, i) for i in between]
    pairs = [(i, i ^ 1) for i in range(blocks)]

    def swap(near, away):
        near = lax.ppermute(near, "rows", pairs)
        return near, lax.ppermute(away, "rows", far)

    held = lax.all_to_all(spread_chunks(slc, pair_index, core), "acq", 0, 0)
    first_halo = swap(*edge_rows_first(slc, core))
    second = lax.all_to_all(pick_chunks(held), "acq", 0, 0)
    second_halo = swap(*edge_rows_second(second, core))
    half_spectrum, edge_sums, coherence = own_part(slc, second, band, right)
    return with_edges(
        half_spectrum, edge_sums, coherence, first_halo + second_halo,
        core, right, right_inv, left, left_inv, band, mean,
    )


def solution(mesh):
    return jax.shard_map(
        on_device,
        mesh=mesh,
        in_specs=(P("acq", None, "rows", None), P("acq", None)),
        out_specs=P("acq", None, "rows", None),
        check_vma=False,
    )
```

```python
import functools

import jax
import jax.numpy as jnp
import ml_dtypes
import numpy as np
from jax import lax
from jax.experimental import pallas as pl
from jax.experimental.pallas import tpu as pltpu
from jax.sharding import PartitionSpec as P

LOOK_R = 5
LOOK_C = 19
PATCH = 32
LANES = 128
BLOCK = 256
OWN_GROUP = 16
LATE_GROUPS = 4
EARLY_GROUPS = 4
EDGE_GROUP = 8
OUT_TILES = 4
VMEM = pl.BlockSpec(memory_space=pltpu.VMEM)
SMEM = pl.BlockSpec(memory_space=pltpu.SMEM)
PARAMS = pltpu.CompilerParams(vmem_limit_bytes=40 * 1024 * 1024)
F32 = jnp.float32
BF16 = jnp.bfloat16


def cost(flops, moved):
    return pl.CostEstimate(flops=flops, bytes_accessed=moved, transcendentals=0)


def halves(matrix):
    high = matrix.astype(ml_dtypes.bfloat16)
    low = (matrix - high.astype(np.float64)).astype(ml_dtypes.bfloat16)
    return high, low


def split(x):
    high = x.astype(BF16)
    low = (x - high.astype(F32)).astype(BF16)
    return high, low


def constants():
    index = np.arange(PATCH)
    phase = 2.0 * np.pi / PATCH * (index[:, None] * index[None, :] % PATCH)
    c, s = np.cos(phase), np.sin(phase)
    eye = np.eye(LANES // PATCH)
    cb, sb = np.kron(eye, c), np.kron(eye, s)

    def three_rows(m):
        h, l = halves(m)
        return np.concatenate([h, h, l], axis=0)

    def three_cols(m):
        h, l = halves(m)
        return np.concatenate([h, h, l], axis=1)

    right = three_rows(np.block([[cb, -sb], [sb, cb]]))
    right_inv = three_rows(np.block([[cb, sb], [-sb, cb]]) / (PATCH * PATCH))
    left = three_cols(np.block([[c, s], [-s, c]]))
    left_inv = three_cols(np.block([[c, -s], [s, c]]))
    half = LOOK_C // 2
    row, col = np.arange(BLOCK)[:, None], np.arange(BLOCK)[None, :]
    near = (np.abs(row - LANES - col) <= half).astype(ml_dtypes.bfloat16)
    far = (np.abs(row + LANES - col) <= half).astype(ml_dtypes.bfloat16)
    band = np.concatenate([near, near, far, far], axis=0)
    mean = np.kron(np.eye(BLOCK // PATCH), np.full((PATCH, PATCH), 1.0 / (PATCH * PATCH))).astype(ml_dtypes.bfloat16)
    mean = np.concatenate([mean, mean], axis=0)
    return right, right_inv, left, left_inv, band, mean


def spread_chunks(slc, pair_index, core):
    count = slc.shape[3] // BLOCK

    def kernel(core_ref, x_ref, pair_ref, o_ref, wanted_ref, held_ref, pair_sem, in_sem, out_sem):
        pair_copy = pltpu.make_async_copy(pair_ref, wanted_ref, pair_sem)
        pair_copy.start()

        def start(first, last, sem):
            for j in range(first, last):
                for k in range(2):
                    cols = slice(BLOCK * j + LANES * k, BLOCK * j + LANES * (k + 1))
                    for c in range(2):
                        rows = slice(64 * k + 32 * c, 64 * k + 32 * c + 32)
                        pltpu.make_async_copy(x_ref.at[0, c, :, cols], held_ref.at[j, rows], sem).start()

        def wait(first, last, sem):
            part = held_ref.at[first:last, 0:128]
            pltpu.make_async_copy(part, part, sem).wait()

        def out(first, last, sem):
            return pltpu.make_async_copy(held_ref.at[first:last], o_ref.at[first:last], sem)

        def fill():
            pair_copy.wait()
            wanted = jnp.full((8, LANES), wanted_ref[0, 1].astype(F32))
            for j in range(count):
                held_ref[j, 128:136] = wanted

        @pl.when(core_ref[0] == 0)
        def _():
            n = count // LATE_GROUPS
            for g in range(LATE_GROUPS):
                start(g * n, g * n + n, in_sem.at[g])
                if g == 0:
                    fill()
                wait(g * n, g * n + n, in_sem.at[g])
                copy = out(g * n, g * n + n, out_sem.at[g])
                copy.start()
                copy.wait()

        @pl.when(core_ref[0] != 0)
        def _():
            n = count // EARLY_GROUPS
            for g in range(EARLY_GROUPS):
                start(g * n, g * n + n, in_sem.at[g])
            fill()
            copies = [out(g * n, g * n + n, out_sem.at[g]) for g in range(EARLY_GROUPS)]
            for g in range(EARLY_GROUPS):
                wait(g * n, g * n + n, in_sem.at[g])
                copies[g].start()
            for copy in copies:
                copy.wait()

    hbm = pl.BlockSpec(memory_space=pltpu.HBM)
    return pl.pallas_call(
        kernel,
        out_shape=jax.ShapeDtypeStruct((count, 136, LANES), F32),
        in_specs=[SMEM, hbm, hbm],
        out_specs=hbm,
        scratch_shapes=[
            pltpu.SMEM((1, 2), jnp.int32),
            pltpu.VMEM((count, 136, LANES), F32),
            pltpu.SemaphoreType.DMA,
            pltpu.SemaphoreType.DMA((max(LATE_GROUPS, EARLY_GROUPS),)),
            pltpu.SemaphoreType.DMA((max(LATE_GROUPS, EARLY_GROUPS),)),
        ],
        compiler_params=pltpu.CompilerParams(vmem_limit_bytes=60 * 1024 * 1024),
        cost_estimate=cost(0, 2 << 20),
        name="spread_chunks",
    )(core, slc, pair_index)


def pick_chunks(held):
    count = held.shape[0]

    def kernel(v_ref, o_ref):
        for p in range(count):
            wanted = v_ref[p, 128:129, 0:1][0, 0].astype(jnp.int32)
            o_ref[p] = v_ref[wanted, 0:128]

    return pl.pallas_call(
        kernel,
        out_shape=jax.ShapeDtypeStruct((count, 128, LANES), F32),
        in_specs=[VMEM],
        out_specs=VMEM,
        compiler_params=PARAMS,
        cost_estimate=cost(0, 2 << 20),
        name="pick_chunks",
    )(held)


def first_sides(core, top, low):
    return jnp.where(core == 0, low, top), jnp.where(core == 0, top, low)


def edge_rows(slc, second, core, mark, near):
    count = second.shape[0]

    def kernel(core_ref, a_ref, b_ref, mark_ref, o_ref):
        pick = 0 if near else 1
        for j in range(count):
            for k in range(2):
                cols = slice(BLOCK * j + LANES * k, BLOCK * j + LANES * (k + 1))
                for c in range(2):
                    at = slice(4 * c + 2 * k, 4 * c + 2 * k + 2)
                    base = 64 * k + 32 * c
                    o_ref[0, j, at] = first_sides(core_ref[0], a_ref[0, c, 0:2, cols], a_ref[0, c, 30:32, cols])[pick]
                    o_ref[1, j, at] = first_sides(core_ref[0], b_ref[j, base : base + 2], b_ref[j, base + 30 : base + 32])[pick]

    return pl.pallas_call(
        kernel,
        out_shape=jax.ShapeDtypeStruct((2, count, 8, LANES), F32),
        in_specs=[SMEM, VMEM, VMEM, VMEM],
        out_specs=VMEM,
        compiler_params=PARAMS,
        cost_estimate=cost(0, 1 << 20),
        name="edge_rows_near" if near else "edge_rows_away",
    )(core, slc, second, mark)


def gamma_of(total):
    scale = lax.rsqrt(total[2] * total[3] + 1e-06)
    gr, gi = total[0] * scale, total[1] * scale
    return gr, gi, jnp.sqrt(gr * gr + gi * gi)


def put_tiles(ref, j, real, imag):
    for k in range(2):
        cols = slice(LANES * k, LANES * (k + 1))
        ref[2 * j + k, :, 0:LANES] = real[:, cols]
        ref[2 * j + k, :, LANES:BLOCK] = imag[:, cols]


def get_tiles(ref, j):
    real = jnp.concatenate([ref[2 * j, :, 0:LANES], ref[2 * j + 1, :, 0:LANES]], axis=1)
    imag = jnp.concatenate([ref[2 * j, :, LANES:BLOCK], ref[2 * j + 1, :, LANES:BLOCK]], axis=1)
    return jnp.concatenate([real, imag], axis=0)


def box_columns(high_ref, low_ref, band, start, n):
    rows = n * high_ref.shape[1]
    parts = [ref[start + d : start + d + n].reshape(rows, BLOCK) for d in range(2) for ref in (high_ref, low_ref)]
    return jnp.dot(jnp.concatenate(parts, axis=1), band, preferred_element_type=F32)


def staggered(count, group, stages):
    starts = list(range(0, count, group))
    for t in range(len(starts) + len(stages) - 1):
        for s in reversed(range(len(stages))):
            if 0 <= t - s < len(starts):
                stages[s](starts[t - s])


def own_part(slc, second, core, turn, band, right):
    count = second.shape[0]
    group = OWN_GROUP

    def kernel(core_ref, a_ref, b_ref, w_ref, r_ref, y_ref, edge_ref, coh_ref, mark_ref, *scratch):
        mark_ref[...] = jnp.zeros(mark_ref.shape, F32)

        @pl.when(core_ref[0] == turn)
        def _():
            work(a_ref, b_ref, w_ref, r_ref, y_ref, edge_ref, coh_ref, *scratch)

    def work(a_ref, b_ref, w_ref, r_ref, y_ref, edge_ref, coh_ref, rows_ref, high_ref, low_ref, gh_ref, gl_ref):
        zero8 = jnp.zeros((8, LANES), F32)
        for slot in range(8):
            rows_ref[slot, 0:8] = zero8
            rows_ref[slot, 40:48] = zero8
        zero = jnp.zeros((128, LANES), BF16)
        for ref in (high_ref, low_ref):
            ref[0, :, 0:LANES] = zero
            ref[count, :, LANES:BLOCK] = zero
        sub = lax.broadcasted_iota(jnp.int32, (8, BLOCK), 0)
        row = lax.broadcasted_iota(jnp.int32, (32, BLOCK), 0)
        inner = (row >= 2) & (row < 30)

        def row_sums(g):
            for t in range(2 * g + 1 if g else 0, min(2 * (g + group) + 1, 2 * count)):
                j, k = t // 2, t % 2
                cols = slice(LANES * t, LANES * (t + 1))
                a0, a1 = a_ref[0, 0, :, cols], a_ref[0, 1, :, cols]
                b0, b1 = b_ref[j, 64 * k : 64 * k + 32], b_ref[j, 64 * k + 32 : 64 * k + 64]
                fields = (a0 * b0 + a1 * b1, a1 * b0 - a0 * b1, a0 * a0 + a1 * a1, b0 * b0 + b1 * b1)
                at, side = (t + 1) // 2, (t + 1) % 2
                lanes = slice(LANES * side, LANES * (side + 1))
                for f, field in enumerate(fields):
                    slot = 4 * (t % 2) + f
                    rows_ref[slot, 8:40] = field
                    total = field
                    for shift in (6, 7, 9, 10):
                        total = total + rows_ref[slot, shift : shift + 32]
                    high, low = split(total)
                    high_ref[at, 32 * f : 32 * f + 32, lanes] = high
                    low_ref[at, 32 * f : 32 * f + 32, lanes] = low

        def gamma(g):
            sums = box_columns(high_ref, low_ref, w_ref[...], g, group)
            for j in range(g, g + group):
                total = [sums[128 * (j - g) + 32 * f : 128 * (j - g) + 32 * f + 32] for f in range(4)]
                for f in range(4):
                    edge_ref[j, 8 * f : 8 * f + 8] = jnp.where(sub < 4, total[f][0:8], total[f][24:32])
                gr, gi, coherence = gamma_of(total)
                coh_ref[:, BLOCK * j : BLOCK * (j + 1)] = coherence
                gr, gi = jnp.where(inner, gr, 0.0), jnp.where(inner, gi, 0.0)
                rh, rl = split(gr)
                ih, il = split(gi)
                put_tiles(gh_ref, j, rh, ih)
                put_tiles(gl_ref, j, rl, il)

        def transform(g):
            m, n = 2 * g, 2 * group
            h, l = (ref[m : m + n].reshape(32 * n, BLOCK) for ref in (gh_ref, gl_ref))
            y = jnp.dot(jnp.concatenate([h, l, h], axis=1), r_ref[...], preferred_element_type=F32)
            y_ref[m : m + n] = y.reshape(n, 32, BLOCK)

        staggered(count, group, (row_sums, gamma, transform))

    return pl.pallas_call(
        kernel,
        out_shape=(
            jax.ShapeDtypeStruct((2 * count, 32, BLOCK), F32),
            jax.ShapeDtypeStruct((count, 32, BLOCK), F32),
            jax.ShapeDtypeStruct((32, BLOCK * count), F32),
            jax.ShapeDtypeStruct((8, LANES), F32),
        ),
        in_specs=[SMEM] + [VMEM] * 4,
        out_specs=(VMEM, VMEM, VMEM, VMEM),
        scratch_shapes=[
            pltpu.VMEM((8, 48, LANES), F32),
            pltpu.VMEM((count + 1, 128, BLOCK), BF16),
            pltpu.VMEM((count + 1, 128, BLOCK), BF16),
            pltpu.VMEM((2 * count, 32, BLOCK), BF16),
            pltpu.VMEM((2 * count, 32, BLOCK), BF16),
        ],
        compiler_params=PARAMS,
        cost_estimate=cost(4 << 30, 12 << 20),
        name="own_part",
    )(core, slc, second, band, right)


def with_edges(late, early, halos, core, right, right_inv, left, left_inv, band, mean):
    count = late[1].shape[0]
    group = EDGE_GROUP

    def kernel(core_ref, *refs):
        @pl.when(core_ref[0] == 0)
        def _():
            work(True, *refs[0:3], *refs[6:])

        @pl.when(core_ref[0] != 0)
        def _():
            work(False, *refs[3:])

    def work(even, yin_ref, edge_ref, coh_ref, near_ref, away_ref,
             r_ref, ri_ref, l_ref, li_ref, w_ref, m_ref, o_ref,
             part_ref, high_ref, low_ref, g_ref, y_ref, z_ref, vh_ref, vl_ref, strip_ref, out_ref, sem):
        copies = [pltpu.make_async_copy(coh_ref.at[8:24], o_ref.at[0, 0, 8:24], sem.at[0])]
        copies[0].start()
        odd_row = lax.broadcasted_iota(jnp.int32, (8, LANES), 0) % 2 == 1
        sub = lax.broadcasted_iota(jnp.int32, (8, BLOCK), 0)
        outer = (sub < 2) | (sub >= 6)
        part_ref[...] = jnp.zeros(part_ref.shape, F32)
        for j in range(count):
            for place in range(2):
                a, b = (
                    near_ref[i, j] if even == (place == 1) else away_ref[i, j]
                    for i in range(2)
                )
                mixed = a * pltpu.roll(b, 4, 0)
                same, aa, bb = a * b, a * a, b * b
                fields = (
                    same + pltpu.roll(same, 4, 0),
                    pltpu.roll(mixed, 4, 0) - mixed,
                    aa + pltpu.roll(aa, 4, 0),
                    bb + pltpu.roll(bb, 4, 0),
                )
                for f, field in enumerate(fields):
                    if place == 0:
                        field = jnp.where(odd_row, field, field + pltpu.roll(field, 7, 0))
                    else:
                        field = jnp.where(odd_row, field + pltpu.roll(field, 1, 0), field)
                    row = 8 * f + 6 * place
                    part_ref[j, row : row + 2, LANES:BLOCK] = field[0:2]
                    part_ref[j + 1, row : row + 2, 0:LANES] = field[2:4]
        for j in range(count + 1):
            high_ref[j], low_ref[j] = split(part_ref[j])

        def gamma(g):
            more = box_columns(high_ref, low_ref, w_ref[...], g, group)
            for j in range(g, g + group):
                at = 32 * (j - g)
                total = [edge_ref[j, 8 * f : 8 * f + 8] + more[at + 8 * f : at + 8 * f + 8] for f in range(4)]
                gr, gi, coherence = gamma_of(total)
                cols = slice(BLOCK * j, BLOCK * (j + 1))
                strip_ref[0, :, cols] = jnp.where(sub < 2, coherence, coh_ref[0:8, cols])
                strip_ref[1, :, cols] = jnp.where(sub >= 6, coherence, coh_ref[24:32, cols])
                put_tiles(g_ref, j, jnp.where(outer, gr, 0.0), jnp.where(outer, gi, 0.0))

        def transform(g):
            m, n = 2 * g, 2 * group
            h, l = split(g_ref[m : m + n].reshape(8 * n, BLOCK))
            y = jnp.dot(jnp.concatenate([h, l, h], axis=1), r_ref[...], preferred_element_type=F32)
            for t in range(n):
                more = y[8 * t : 8 * t + 8]
                y_ref[m + t, 0:8] = yin_ref[m + t, 0:8] + jnp.where(sub < 4, more, 0.0)
                y_ref[m + t, 8:24] = yin_ref[m + t, 8:24]
                y_ref[m + t, 24:32] = yin_ref[m + t, 24:32] + jnp.where(sub < 4, 0.0, more)

        def forward(g):
            for j in range(g, g + group):
                h, l = split(get_tiles(y_ref, j))
                z_ref[j] = jnp.dot(l_ref[...], jnp.concatenate([h, l, h], axis=0), preferred_element_type=F32)

        sums = {}

        def backward(g):
            parts = []
            for j in range(g, g + group):
                zr, zi = z_ref[j, 0:32], z_ref[j, 32:64]
                weight = lax.rsqrt(lax.rsqrt(zr * zr + zi * zi + 1e-06))
                parts.append(weight[0:8] + weight[8:16] + weight[16:24] + weight[24:32])
                h, l = split(jnp.concatenate([zr * weight, zi * weight], axis=0))
                v = jnp.dot(li_ref[...], jnp.concatenate([h, l, h], axis=0), preferred_element_type=F32)
                h, l = split(v)
                put_tiles(vh_ref, j, h[0:32], h[32:64])
                put_tiles(vl_ref, j, l[0:32], l[32:64])
            h, l = split(jnp.concatenate(parts, axis=0))
            total = jnp.dot(jnp.concatenate([h, l], axis=1), m_ref[...], preferred_element_type=F32)
            sums[g] = 1.0 / jnp.sum(total.reshape(group, 8, BLOCK), axis=1, keepdims=True)

        def finish(g):
            m, n = 2 * g, 2 * group
            h, l = (ref[m : m + n].reshape(32 * n, BLOCK) for ref in (vh_ref, vl_ref))
            out = jnp.dot(jnp.concatenate([h, l, h], axis=1), ri_ref[...], preferred_element_type=F32)
            for t in range(n):
                factor = sums[g][t // 2, :, LANES * (t % 2) : LANES * (t % 2 + 1)]
                cols = slice(LANES * (m + t), LANES * (m + t + 1))
                out_ref[0, :, cols] = out[32 * t : 32 * t + 32, 0:LANES] * factor
                out_ref[1, :, cols] = out[32 * t : 32 * t + 32, LANES:BLOCK] * factor
                if (t + 1) % OUT_TILES == 0:
                    cols = slice(LANES * (m + t + 1 - OUT_TILES), LANES * (m + t + 1))
                    at = sem.at[3 + (m + t) // OUT_TILES]
                    copy = pltpu.make_async_copy(out_ref.at[:, :, cols], o_ref.at[0, 1:3, :, cols], at)
                    copy.start()
                    copies.append(copy)
            if g + group == count:
                for i in range(2):
                    copy = pltpu.make_async_copy(strip_ref.at[i], o_ref.at[0, 0, 24 * i : 24 * i + 8], sem.at[1 + i])
                    copy.start()
                    copies.append(copy)

        staggered(count, group, (gamma, transform, forward, backward, finish))
        for copy in copies:
            copy.wait()

    return pl.pallas_call(
        kernel,
        out_shape=jax.ShapeDtypeStruct((1, 3, 32, BLOCK * count), F32),
        in_specs=[SMEM] + [VMEM] * 14,
        out_specs=pl.BlockSpec(memory_space=pltpu.HBM),
        scratch_shapes=[
            pltpu.VMEM((count + 1, 32, BLOCK), F32),
            pltpu.VMEM((count + 1, 32, BLOCK), BF16),
            pltpu.VMEM((count + 1, 32, BLOCK), BF16),
            pltpu.VMEM((2 * count, 8, BLOCK), F32),
            pltpu.VMEM((2 * count, 32, BLOCK), F32),
            pltpu.VMEM((count, 64, BLOCK), F32),
            pltpu.VMEM((2 * count, 32, BLOCK), BF16),
            pltpu.VMEM((2 * count, 32, BLOCK), BF16),
            pltpu.VMEM((2, 8, BLOCK * count), F32),
            pltpu.VMEM((2, 32, BLOCK * count), F32),
            pltpu.SemaphoreType.DMA((3 + 2 * count // OUT_TILES,)),
        ],
        compiler_params=PARAMS,
        cost_estimate=cost(8 << 30, 8 << 20),
        name="with_edges",
    )(core, *late, *early, *halos, right, right_inv, left, left_inv, band, mean)


def on_device(slc, pair_index):
    right, right_inv, left, left_inv, band, mean = (jnp.asarray(m) for m in constants())
    blocks = lax.axis_size("rows")
    core = (lax.axis_index("rows") % 2).astype(jnp.int32).reshape(1)
    between = range(1, blocks - 1, 2)
    far = [(i, i + 1) for i in between] + [(i + 1, i) for i in between]
    pairs = [(i, i ^ 1) for i in range(blocks)]

    held = lax.all_to_all(spread_chunks(slc, pair_index, core), "acq", 0, 0)
    second = lax.all_to_all(pick_chunks(held), "acq", 0, 0)
    *early, mark = own_part(slc, second, core, 1, band, right)
    away = lax.ppermute(edge_rows(slc, second, core, mark, False), "rows", far)
    *late, mark = own_part(slc, second, core, 0, band, right)
    near = lax.ppermute(edge_rows(slc, second, core, mark, True), "rows", pairs)
    return with_edges(
        late, early, (near, away), core, right, right_inv, left, left_inv, band, mean,
    )


def solution(mesh):
    return jax.shard_map(
        on_device,
        mesh=mesh,
        in_specs=(P("acq", None, "rows", None), P("acq", None)),
        out_specs=P("acq", None, "rows", None),
        check_vma=False,
    )
```

```python
import functools

import jax
import jax.numpy as jnp
import ml_dtypes
import numpy as np
from jax import lax
from jax.experimental import pallas as pl
from jax.experimental.pallas import tpu as pltpu
from jax.sharding import PartitionSpec as P

LOOK_R = 5
LOOK_C = 19
PATCH = 32
LANES = 128
BLOCK = 256
OWN_GROUP = 16
LATE_GROUPS = 3
EARLY_GROUPS = 4
EDGE_GROUP = 8
OUT_TILES = 2
VMEM = pl.BlockSpec(memory_space=pltpu.VMEM)
SMEM = pl.BlockSpec(memory_space=pltpu.SMEM)
PARAMS = pltpu.CompilerParams(vmem_limit_bytes=40 * 1024 * 1024)
F32 = jnp.float32
BF16 = jnp.bfloat16


def cost(flops, moved):
    return pl.CostEstimate(flops=flops, bytes_accessed=moved, transcendentals=0)


def halves(matrix):
    high = matrix.astype(ml_dtypes.bfloat16)
    low = (matrix - high.astype(np.float64)).astype(ml_dtypes.bfloat16)
    return high, low


def split(x):
    high = x.astype(BF16)
    low = (x - high.astype(F32)).astype(BF16)
    return high, low


def constants():
    index = np.arange(PATCH)
    phase = 2.0 * np.pi / PATCH * (index[:, None] * index[None, :] % PATCH)
    c, s = np.cos(phase), np.sin(phase)
    eye = np.eye(LANES // PATCH)
    cb, sb = np.kron(eye, c), np.kron(eye, s)

    def three_rows(m):
        h, l = halves(m)
        return np.concatenate([h, h, l], axis=0)

    def three_cols(m):
        h, l = halves(m)
        return np.concatenate([h, h, l], axis=1)

    right = three_rows(np.block([[cb, -sb], [sb, cb]]))
    right_inv = three_rows(np.block([[cb, sb], [-sb, cb]]) / (PATCH * PATCH))
    left = three_cols(np.block([[c, s], [-s, c]]))
    left_inv = three_cols(np.block([[c, -s], [s, c]]))
    half = LOOK_C // 2
    row, col = np.arange(BLOCK)[:, None], np.arange(BLOCK)[None, :]
    near = (np.abs(row - LANES - col) <= half).astype(ml_dtypes.bfloat16)
    far = (np.abs(row + LANES - col) <= half).astype(ml_dtypes.bfloat16)
    band = np.concatenate([near, near, far, far], axis=0)
    mean = np.kron(np.eye(BLOCK // PATCH), np.full((PATCH, PATCH), 1.0 / (PATCH * PATCH))).astype(ml_dtypes.bfloat16)
    mean = np.concatenate([mean, mean], axis=0)
    return right, right_inv, left, left_inv, band, mean


def spread_chunks(slc, pair_index, core):
    count = slc.shape[3] // BLOCK

    def kernel(core_ref, x_ref, pair_ref, o_ref, wanted_ref, held_ref, pair_sem, in_sem, out_sem):
        pair_copy = pltpu.make_async_copy(pair_ref, wanted_ref, pair_sem)
        pair_copy.start()

        def start(first, last, sem):
            for j in range(first, last):
                for k in range(2):
                    cols = slice(BLOCK * j + LANES * k, BLOCK * j + LANES * (k + 1))
                    for c in range(2):
                        rows = slice(64 * k + 32 * c, 64 * k + 32 * c + 32)
                        pltpu.make_async_copy(x_ref.at[0, c, :, cols], held_ref.at[j, rows], sem).start()

        def wait(first, last, sem):
            part = held_ref.at[first:last, 0:128]
            pltpu.make_async_copy(part, part, sem).wait()

        def out(first, last, sem):
            return pltpu.make_async_copy(held_ref.at[first:last], o_ref.at[first:last], sem)

        def fill():
            pair_copy.wait()
            wanted = jnp.full((8, LANES), wanted_ref[0, 1].astype(F32))
            for j in range(count):
                held_ref[j, 128:136] = wanted

        @pl.when(core_ref[0] == 0)
        def _():
            ends = [count * (g + 1) // LATE_GROUPS for g in range(LATE_GROUPS)]
            for g, (first, last) in enumerate(zip([0] + ends, ends)):
                start(first, last, in_sem.at[g])
                if g == 0:
                    fill()
                wait(first, last, in_sem.at[g])
                copy = out(first, last, out_sem.at[g])
                copy.start()
                copy.wait()

        @pl.when(core_ref[0] != 0)
        def _():
            n = count // EARLY_GROUPS
            copies = []

            def send(groups, rows, sem):
                copy = pltpu.make_async_copy(held_ref.at[groups, rows], o_ref.at[groups, rows], sem)
                copy.start()
                copies.append(copy)

            for g in range(EARLY_GROUPS):
                start(g * n, g * n + n, in_sem.at[g])
            for g in range(EARLY_GROUPS):
                wait(g * n, g * n + n, in_sem.at[g])
                send(slice(g * n, g * n + n), slice(0, 128), out_sem.at[g])
            fill()
            send(slice(0, count), slice(128, 136), out_sem.at[EARLY_GROUPS])
            for copy in copies:
                copy.wait()

    hbm = pl.BlockSpec(memory_space=pltpu.HBM)
    return pl.pallas_call(
        kernel,
        out_shape=jax.ShapeDtypeStruct((count, 136, LANES), F32),
        in_specs=[SMEM, hbm, hbm],
        out_specs=hbm,
        scratch_shapes=[
            pltpu.SMEM((1, 2), jnp.int32),
            pltpu.VMEM((count, 136, LANES), F32),
            pltpu.SemaphoreType.DMA,
            pltpu.SemaphoreType.DMA((max(LATE_GROUPS, EARLY_GROUPS),)),
            pltpu.SemaphoreType.DMA((max(LATE_GROUPS, EARLY_GROUPS + 1),)),
        ],
        compiler_params=pltpu.CompilerParams(vmem_limit_bytes=60 * 1024 * 1024),
        cost_estimate=cost(0, 2 << 20),
        name="spread_chunks",
    )(core, slc, pair_index)


def pick_chunks(held):
    count = held.shape[0]

    def kernel(v_ref, o_ref):
        for p in range(count):
            wanted = v_ref[p, 128:129, 0:1][0, 0].astype(jnp.int32)
            o_ref[p] = v_ref[wanted, 0:128]

    return pl.pallas_call(
        kernel,
        out_shape=jax.ShapeDtypeStruct((count, 128, LANES), F32),
        in_specs=[VMEM],
        out_specs=VMEM,
        compiler_params=PARAMS,
        cost_estimate=cost(0, 2 << 20),
        name="pick_chunks",
    )(held)


def first_sides(core, top, low):
    return jnp.where(core == 0, low, top), jnp.where(core == 0, top, low)


def edge_rows(slc, second, core, mark, near):
    count = second.shape[0]

    def kernel(core_ref, a_ref, b_ref, mark_ref, o_ref):
        pick = 0 if near else 1
        for j in range(count):
            for k in range(2):
                cols = slice(BLOCK * j + LANES * k, BLOCK * j + LANES * (k + 1))
                for c in range(2):
                    at = slice(4 * c + 2 * k, 4 * c + 2 * k + 2)
                    base = 64 * k + 32 * c
                    o_ref[0, j, at] = first_sides(core_ref[0], a_ref[0, c, 0:2, cols], a_ref[0, c, 30:32, cols])[pick]
                    o_ref[1, j, at] = first_sides(core_ref[0], b_ref[j, base : base + 2], b_ref[j, base + 30 : base + 32])[pick]

    return pl.pallas_call(
        kernel,
        out_shape=jax.ShapeDtypeStruct((2, count, 8, LANES), F32),
        in_specs=[SMEM, VMEM, VMEM, VMEM],
        out_specs=VMEM,
        compiler_params=PARAMS,
        cost_estimate=cost(0, 1 << 20),
        name="edge_rows_near" if near else "edge_rows_away",
    )(core, slc, second, mark)


def gamma_of(total):
    scale = lax.rsqrt(total[2] * total[3] + 1e-06)
    gr, gi = total[0] * scale, total[1] * scale
    return gr, gi, jnp.sqrt(gr * gr + gi * gi)


def put_tiles(ref, j, real, imag):
    for k in range(2):
        cols = slice(LANES * k, LANES * (k + 1))
        ref[2 * j + k, :, 0:LANES] = real[:, cols]
        ref[2 * j + k, :, LANES:BLOCK] = imag[:, cols]


def get_tiles(ref, j):
    real = jnp.concatenate([ref[2 * j, :, 0:LANES], ref[2 * j + 1, :, 0:LANES]], axis=1)
    imag = jnp.concatenate([ref[2 * j, :, LANES:BLOCK], ref[2 * j + 1, :, LANES:BLOCK]], axis=1)
    return jnp.concatenate([real, imag], axis=0)


def box_columns(high_ref, low_ref, band, start, n):
    rows = n * high_ref.shape[1]
    parts = [ref[start + d : start + d + n].reshape(rows, BLOCK) for d in range(2) for ref in (high_ref, low_ref)]
    return jnp.dot(jnp.concatenate(parts, axis=1), band, preferred_element_type=F32)


def staggered(count, group, stages):
    starts = list(range(0, count, group))
    for t in range(len(starts) + len(stages) - 1):
        for s in reversed(range(len(stages))):
            if 0 <= t - s < len(starts):
                stages[s](starts[t - s])


def own_part(slc, second, core, turn, band, right):
    count = second.shape[0]
    group = OWN_GROUP

    def kernel(core_ref, a_ref, b_ref, w_ref, r_ref, y_ref, edge_ref, coh_ref, mark_ref, *scratch):
        mark_ref[...] = jnp.zeros(mark_ref.shape, F32)

        @pl.when(core_ref[0] == turn)
        def _():
            work(a_ref, b_ref, w_ref, r_ref, y_ref, edge_ref, coh_ref, *scratch)

    def work(a_ref, b_ref, w_ref, r_ref, y_ref, edge_ref, coh_ref, rows_ref, high_ref, low_ref, gh_ref, gl_ref):
        zero8 = jnp.zeros((8, LANES), F32)
        for slot in range(8):
            rows_ref[slot, 0:8] = zero8
            rows_ref[slot, 40:48] = zero8
        zero = jnp.zeros((128, LANES), BF16)
        for ref in (high_ref, low_ref):
            ref[0, :, 0:LANES] = zero
            ref[count, :, LANES:BLOCK] = zero
        sub = lax.broadcasted_iota(jnp.int32, (8, BLOCK), 0)
        row = lax.broadcasted_iota(jnp.int32, (32, BLOCK), 0)
        inner = (row >= 2) & (row < 30)

        def row_sums(g):
            for t in range(2 * g + 1 if g else 0, min(2 * (g + group) + 1, 2 * count)):
                j, k = t // 2, t % 2
                cols = slice(LANES * t, LANES * (t + 1))
                a0, a1 = a_ref[0, 0, :, cols], a_ref[0, 1, :, cols]
                b0, b1 = b_ref[j, 64 * k : 64 * k + 32], b_ref[j, 64 * k + 32 : 64 * k + 64]
                fields = (a0 * b0 + a1 * b1, a1 * b0 - a0 * b1, a0 * a0 + a1 * a1, b0 * b0 + b1 * b1)
                at, side = (t + 1) // 2, (t + 1) % 2
                lanes = slice(LANES * side, LANES * (side + 1))
                for f, field in enumerate(fields):
                    slot = 4 * (t % 2) + f
                    rows_ref[slot, 8:40] = field
                    total = field
                    for shift in (6, 7, 9, 10):
                        total = total + rows_ref[slot, shift : shift + 32]
                    high, low = split(total)
                    high_ref[at, 32 * f : 32 * f + 32, lanes] = high
                    low_ref[at, 32 * f : 32 * f + 32, lanes] = low

        def gamma(g):
            sums = box_columns(high_ref, low_ref, w_ref[...], g, group)
            for j in range(g, g + group):
                total = [sums[128 * (j - g) + 32 * f : 128 * (j - g) + 32 * f + 32] for f in range(4)]
                for f in range(4):
                    edge_ref[j, 8 * f : 8 * f + 8] = jnp.where(sub < 4, total[f][0:8], total[f][24:32])
                gr, gi, coherence = gamma_of(total)
                coh_ref[:, BLOCK * j : BLOCK * (j + 1)] = coherence
                gr, gi = jnp.where(inner, gr, 0.0), jnp.where(inner, gi, 0.0)
                rh, rl = split(gr)
                ih, il = split(gi)
                put_tiles(gh_ref, j, rh, ih)
                put_tiles(gl_ref, j, rl, il)

        def transform(g):
            m, n = 2 * g, 2 * group
            h, l = (ref[m : m + n].reshape(32 * n, BLOCK) for ref in (gh_ref, gl_ref))
            y = jnp.dot(jnp.concatenate([h, l, h], axis=1), r_ref[...], preferred_element_type=F32)
            y_ref[m : m + n] = y.reshape(n, 32, BLOCK)

        staggered(count, group, (row_sums, gamma, transform))

    return pl.pallas_call(
        kernel,
        out_shape=(
            jax.ShapeDtypeStruct((2 * count, 32, BLOCK), F32),
            jax.ShapeDtypeStruct((count, 32, BLOCK), F32),
            jax.ShapeDtypeStruct((32, BLOCK * count), F32),
            jax.ShapeDtypeStruct((8, LANES), F32),
        ),
        in_specs=[SMEM] + [VMEM] * 4,
        out_specs=(VMEM, VMEM, VMEM, VMEM),
        scratch_shapes=[
            pltpu.VMEM((8, 48, LANES), F32),
            pltpu.VMEM((count + 1, 128, BLOCK), BF16),
            pltpu.VMEM((count + 1, 128, BLOCK), BF16),
            pltpu.VMEM((2 * count, 32, BLOCK), BF16),
            pltpu.VMEM((2 * count, 32, BLOCK), BF16),
        ],
        compiler_params=PARAMS,
        cost_estimate=cost(4 << 30, 12 << 20),
        name="own_part",
    )(core, slc, second, band, right)


def with_edges(late, early, halos, core, right, right_inv, left, left_inv, band, mean):
    count = late[1].shape[0]
    group = EDGE_GROUP

    def kernel(core_ref, *refs):
        @pl.when(core_ref[0] == 0)
        def _():
            work(True, *refs[0:3], *refs[6:])

        @pl.when(core_ref[0] != 0)
        def _():
            work(False, *refs[3:])

    def work(even, yin_ref, edge_ref, coh_ref, near_ref, away_ref,
             r_ref, ri_ref, l_ref, li_ref, w_ref, m_ref, o_ref,
             part_ref, high_ref, low_ref, g_ref, y_ref, z_ref, vh_ref, vl_ref, strip_ref, out_ref, sem):
        copies = [pltpu.make_async_copy(coh_ref.at[8:24], o_ref.at[0, 0, 8:24], sem.at[0])]
        copies[0].start()
        odd_row = lax.broadcasted_iota(jnp.int32, (8, LANES), 0) % 2 == 1
        sub = lax.broadcasted_iota(jnp.int32, (8, BLOCK), 0)
        outer = (sub < 2) | (sub >= 6)
        part_ref[...] = jnp.zeros(part_ref.shape, F32)
        for j in range(count):
            for place in range(2):
                a, b = (
                    near_ref[i, j] if even == (place == 1) else away_ref[i, j]
                    for i in range(2)
                )
                mixed = a * pltpu.roll(b, 4, 0)
                same, aa, bb = a * b, a * a, b * b
                fields = (
                    same + pltpu.roll(same, 4, 0),
                    pltpu.roll(mixed, 4, 0) - mixed,
                    aa + pltpu.roll(aa, 4, 0),
                    bb + pltpu.roll(bb, 4, 0),
                )
                for f, field in enumerate(fields):
                    if place == 0:
                        field = jnp.where(odd_row, field, field + pltpu.roll(field, 7, 0))
                    else:
                        field = jnp.where(odd_row, field + pltpu.roll(field, 1, 0), field)
                    row = 8 * f + 6 * place
                    part_ref[j, row : row + 2, LANES:BLOCK] = field[0:2]
                    part_ref[j + 1, row : row + 2, 0:LANES] = field[2:4]
        for j in range(count + 1):
            high_ref[j], low_ref[j] = split(part_ref[j])

        def gamma(g):
            more = box_columns(high_ref, low_ref, w_ref[...], g, group)
            for j in range(g, g + group):
                at = 32 * (j - g)
                total = [edge_ref[j, 8 * f : 8 * f + 8] + more[at + 8 * f : at + 8 * f + 8] for f in range(4)]
                gr, gi, coherence = gamma_of(total)
                cols = slice(BLOCK * j, BLOCK * (j + 1))
                strip_ref[0, :, cols] = jnp.where(sub < 2, coherence, coh_ref[0:8, cols])
                strip_ref[1, :, cols] = jnp.where(sub >= 6, coherence, coh_ref[24:32, cols])
                put_tiles(g_ref, j, jnp.where(outer, gr, 0.0), jnp.where(outer, gi, 0.0))

        def transform(g):
            m, n = 2 * g, 2 * group
            h, l = split(g_ref[m : m + n].reshape(8 * n, BLOCK))
            y = jnp.dot(jnp.concatenate([h, l, h], axis=1), r_ref[...], preferred_element_type=F32)
            for t in range(n):
                more = y[8 * t : 8 * t + 8]
                y_ref[m + t, 0:8] = yin_ref[m + t, 0:8] + jnp.where(sub < 4, more, 0.0)
                y_ref[m + t, 8:24] = yin_ref[m + t, 8:24]
                y_ref[m + t, 24:32] = yin_ref[m + t, 24:32] + jnp.where(sub < 4, 0.0, more)

        def forward(g):
            for j in range(g, g + group):
                h, l = split(get_tiles(y_ref, j))
                z_ref[j] = jnp.dot(l_ref[...], jnp.concatenate([h, l, h], axis=0), preferred_element_type=F32)

        sums = {}

        def backward(g):
            parts = []
            for j in range(g, g + group):
                zr, zi = z_ref[j, 0:32], z_ref[j, 32:64]
                weight = lax.rsqrt(lax.rsqrt(zr * zr + zi * zi + 1e-06))
                parts.append(weight[0:8] + weight[8:16] + weight[16:24] + weight[24:32])
                h, l = split(jnp.concatenate([zr * weight, zi * weight], axis=0))
                v = jnp.dot(li_ref[...], jnp.concatenate([h, l, h], axis=0), preferred_element_type=F32)
                h, l = split(v)
                put_tiles(vh_ref, j, h[0:32], h[32:64])
                put_tiles(vl_ref, j, l[0:32], l[32:64])
            h, l = split(jnp.concatenate(parts, axis=0))
            total = jnp.dot(jnp.concatenate([h, l], axis=1), m_ref[...], preferred_element_type=F32)
            sums[g] = 1.0 / jnp.sum(total.reshape(group, 8, BLOCK), axis=1, keepdims=True)

        def finish(g):
            m, n = 2 * g, 2 * group
            h, l = (ref[m : m + n].reshape(32 * n, BLOCK) for ref in (vh_ref, vl_ref))
            out = jnp.dot(jnp.concatenate([h, l, h], axis=1), ri_ref[...], preferred_element_type=F32)
            for t in range(n):
                factor = sums[g][t // 2, :, LANES * (t % 2) : LANES * (t % 2 + 1)]
                cols = slice(LANES * (m + t), LANES * (m + t + 1))
                out_ref[0, :, cols] = out[32 * t : 32 * t + 32, 0:LANES] * factor
                out_ref[1, :, cols] = out[32 * t : 32 * t + 32, LANES:BLOCK] * factor
                if (t + 1) % OUT_TILES == 0:
                    cols = slice(LANES * (m + t + 1 - OUT_TILES), LANES * (m + t + 1))
                    at = sem.at[3 + (m + t) // OUT_TILES]
                    copy = pltpu.make_async_copy(out_ref.at[:, :, cols], o_ref.at[0, 1:3, :, cols], at)
                    copy.start()
                    copies.append(copy)
            if g + group == count:
                for i in range(2):
                    copy = pltpu.make_async_copy(strip_ref.at[i], o_ref.at[0, 0, 24 * i : 24 * i + 8], sem.at[1 + i])
                    copy.start()
                    copies.append(copy)

        staggered(count, group, (gamma, transform, forward, backward, finish))
        for copy in copies:
            copy.wait()

    return pl.pallas_call(
        kernel,
        out_shape=jax.ShapeDtypeStruct((1, 3, 32, BLOCK * count), F32),
        in_specs=[SMEM] + [VMEM] * 14,
        out_specs=pl.BlockSpec(memory_space=pltpu.HBM),
        scratch_shapes=[
            pltpu.VMEM((count + 1, 32, BLOCK), F32),
            pltpu.VMEM((count + 1, 32, BLOCK), BF16),
            pltpu.VMEM((count + 1, 32, BLOCK), BF16),
            pltpu.VMEM((2 * count, 8, BLOCK), F32),
            pltpu.VMEM((2 * count, 32, BLOCK), F32),
            pltpu.VMEM((count, 64, BLOCK), F32),
            pltpu.VMEM((2 * count, 32, BLOCK), BF16),
            pltpu.VMEM((2 * count, 32, BLOCK), BF16),
            pltpu.VMEM((2, 8, BLOCK * count), F32),
            pltpu.VMEM((2, 32, BLOCK * count), F32),
            pltpu.SemaphoreType.DMA((3 + 2 * count // OUT_TILES,)),
        ],
        compiler_params=PARAMS,
        cost_estimate=cost(8 << 30, 8 << 20),
        name="with_edges",
    )(core, *late, *early, *halos, right, right_inv, left, left_inv, band, mean)


def on_device(slc, pair_index):
    right, right_inv, left, left_inv, band, mean = (jnp.asarray(m) for m in constants())
    blocks = lax.axis_size("rows")
    core = (lax.axis_index("rows") % 2).astype(jnp.int32).reshape(1)
    between = range(1, blocks - 1, 2)
    far = [(i, i + 1) for i in between] + [(i + 1, i) for i in between]
    pairs = [(i, i ^ 1) for i in range(blocks)]

    held = lax.all_to_all(spread_chunks(slc, pair_index, core), "acq", 0, 0)
    second = lax.all_to_all(pick_chunks(held), "acq", 0, 0)
    *early, mark = own_part(slc, second, core, 1, band, right)
    away = lax.ppermute(edge_rows(slc, second, core, mark, False), "rows", far)
    *late, mark = own_part(slc, second, core, 0, band, right)
    near = lax.ppermute(edge_rows(slc, second, core, mark, True), "rows", pairs)
    return with_edges(
        late, early, (near, away), core, right, right_inv, left, left_inv, band, mean,
    )


def solution(mesh):
    return jax.shard_map(
        on_device,
        mesh=mesh,
        in_specs=(P("acq", None, "rows", None), P("acq", None)),
        out_specs=P("acq", None, "rows", None),
        check_vma=False,
    )
```

```python
import functools

import jax
import jax.numpy as jnp
import ml_dtypes
import numpy as np
from jax import lax
from jax.experimental import pallas as pl
from jax.experimental.pallas import tpu as pltpu
from jax.sharding import PartitionSpec as P

LOOK_R = 5
LOOK_C = 19
PATCH = 32
LANES = 128
BLOCK = 256
OWN_GROUP = 16
LATE_GROUPS = 3
EARLY_GROUPS = 4
EDGE_GROUP = 8
OUT_TILES = 2
VMEM = pl.BlockSpec(memory_space=pltpu.VMEM)
SMEM = pl.BlockSpec(memory_space=pltpu.SMEM)
PARAMS = pltpu.CompilerParams(vmem_limit_bytes=40 * 1024 * 1024)
F32 = jnp.float32
BF16 = jnp.bfloat16


def cost(flops, moved):
    return pl.CostEstimate(flops=flops, bytes_accessed=moved, transcendentals=0)


def halves(matrix):
    high = matrix.astype(ml_dtypes.bfloat16)
    low = (matrix - high.astype(np.float64)).astype(ml_dtypes.bfloat16)
    return high, low


def split(x):
    high = x.astype(BF16)
    low = (x - high.astype(F32)).astype(BF16)
    return high, low


def constants():
    index = np.arange(PATCH)
    phase = 2.0 * np.pi / PATCH * (index[:, None] * index[None, :] % PATCH)
    c, s = np.cos(phase), np.sin(phase)
    eye = np.eye(LANES // PATCH)
    cb, sb = np.kron(eye, c), np.kron(eye, s)

    def three_rows(m):
        h, l = halves(m)
        return np.concatenate([h, h, l], axis=0)

    def three_cols(m):
        h, l = halves(m)
        return np.concatenate([h, h, l], axis=1)

    right = three_rows(np.block([[cb, -sb], [sb, cb]]))
    right_inv = three_rows(np.block([[cb, sb], [-sb, cb]]) / (PATCH * PATCH))
    left = three_cols(np.block([[c, s], [-s, c]]))
    left_inv = three_cols(np.block([[c, -s], [s, c]]))
    half = LOOK_C // 2
    row, col = np.arange(BLOCK)[:, None], np.arange(BLOCK)[None, :]
    near = (np.abs(row - LANES - col) <= half).astype(ml_dtypes.bfloat16)
    far = (np.abs(row + LANES - col) <= half).astype(ml_dtypes.bfloat16)
    band = np.concatenate([near, near, far, far], axis=0)
    mean = np.kron(np.eye(BLOCK // PATCH), np.full((PATCH, PATCH), 1.0 / (PATCH * PATCH))).astype(ml_dtypes.bfloat16)
    mean = np.concatenate([mean, mean], axis=0)
    return right, right_inv, left, left_inv, band, mean


def spread_chunks(slc, pair_index, core):
    count = slc.shape[3] // BLOCK

    def kernel(core_ref, x_ref, pair_ref, o_ref, wanted_ref, held_ref, pair_sem, in_sem, out_sem):
        pair_copy = pltpu.make_async_copy(pair_ref, wanted_ref, pair_sem)
        pair_copy.start()

        def start(first, last, sem):
            for j in range(first, last):
                for k in range(2):
                    cols = slice(BLOCK * j + LANES * k, BLOCK * j + LANES * (k + 1))
                    for c in range(2):
                        rows = slice(64 * k + 32 * c, 64 * k + 32 * c + 32)
                        pltpu.make_async_copy(x_ref.at[0, c, :, cols], held_ref.at[j, rows], sem).start()

        def wait(first, last, sem):
            part = held_ref.at[first:last, 0:128]
            pltpu.make_async_copy(part, part, sem).wait()

        def out(first, last, sem):
            return pltpu.make_async_copy(held_ref.at[first:last], o_ref.at[first:last], sem)

        def fill():
            pair_copy.wait()
            wanted = jnp.full((8, LANES), wanted_ref[0, 1].astype(F32))
            for j in range(count):
                held_ref[j, 128:136] = wanted

        @pl.when(core_ref[0] == 0)
        def _():
            ends = [count * (g + 1) // LATE_GROUPS for g in range(LATE_GROUPS)]
            for g, (first, last) in enumerate(zip([0] + ends, ends)):
                start(first, last, in_sem.at[g])
                if g == 0:
                    fill()
                wait(first, last, in_sem.at[g])
                copy = out(first, last, out_sem.at[g])
                copy.start()
                copy.wait()

        @pl.when(core_ref[0] != 0)
        def _():
            n = count // EARLY_GROUPS
            copies = []

            def send(groups, rows, sem):
                copy = pltpu.make_async_copy(held_ref.at[groups, rows], o_ref.at[groups, rows], sem)
                copy.start()
                copies.append(copy)

            for g in range(EARLY_GROUPS):
                start(g * n, g * n + n, in_sem.at[g])
            for g in range(EARLY_GROUPS):
                wait(g * n, g * n + n, in_sem.at[g])
                send(slice(g * n, g * n + n), slice(0, 128), out_sem.at[g])
            fill()
            send(slice(0, count), slice(128, 136), out_sem.at[EARLY_GROUPS])
            for copy in copies:
                copy.wait()

    hbm = pl.BlockSpec(memory_space=pltpu.HBM)
    return pl.pallas_call(
        kernel,
        out_shape=jax.ShapeDtypeStruct((count, 136, LANES), F32),
        in_specs=[SMEM, hbm, hbm],
        out_specs=hbm,
        scratch_shapes=[
            pltpu.SMEM((1, 2), jnp.int32),
            pltpu.VMEM((count, 136, LANES), F32),
            pltpu.SemaphoreType.DMA,
            pltpu.SemaphoreType.DMA((max(LATE_GROUPS, EARLY_GROUPS),)),
            pltpu.SemaphoreType.DMA((max(LATE_GROUPS, EARLY_GROUPS + 1),)),
        ],
        compiler_params=pltpu.CompilerParams(vmem_limit_bytes=60 * 1024 * 1024),
        cost_estimate=cost(0, 2 << 20),
        name="spread_chunks",
    )(core, slc, pair_index)


def pick_chunks(held):
    count = held.shape[0]

    def kernel(v_ref, o_ref):
        for p in range(count):
            wanted = v_ref[p, 128:129, 0:1][0, 0].astype(jnp.int32)
            o_ref[p] = v_ref[wanted, 0:128]

    return pl.pallas_call(
        kernel,
        out_shape=jax.ShapeDtypeStruct((count, 128, LANES), F32),
        in_specs=[VMEM],
        out_specs=VMEM,
        compiler_params=PARAMS,
        cost_estimate=cost(0, 2 << 20),
        name="pick_chunks",
    )(held)


def first_sides(core, top, low):
    return jnp.where(core == 0, low, top), jnp.where(core == 0, top, low)


def edge_rows(slc, second, core, mark, near):
    count = second.shape[0]

    def kernel(core_ref, a_ref, b_ref, mark_ref, o_ref):
        pick = 0 if near else 1
        for j in range(count):
            for k in range(2):
                cols = slice(BLOCK * j + LANES * k, BLOCK * j + LANES * (k + 1))
                for c in range(2):
                    at = slice(4 * c + 2 * k, 4 * c + 2 * k + 2)
                    base = 64 * k + 32 * c
                    o_ref[0, j, at] = first_sides(core_ref[0], a_ref[0, c, 0:2, cols], a_ref[0, c, 30:32, cols])[pick]
                    o_ref[1, j, at] = first_sides(core_ref[0], b_ref[j, base : base + 2], b_ref[j, base + 30 : base + 32])[pick]

    return pl.pallas_call(
        kernel,
        out_shape=jax.ShapeDtypeStruct((2, count, 8, LANES), F32),
        in_specs=[SMEM, VMEM, VMEM, VMEM],
        out_specs=VMEM,
        compiler_params=PARAMS,
        cost_estimate=cost(0, 1 << 20),
        name="edge_rows_near" if near else "edge_rows_away",
    )(core, slc, second, mark)


def gamma_of(total):
    scale = lax.rsqrt(total[2] * total[3] + 1e-06)
    gr, gi = total[0] * scale, total[1] * scale
    return gr, gi, jnp.sqrt(gr * gr + gi * gi)


def put_tiles(ref, j, real, imag):
    for k in range(2):
        cols = slice(LANES * k, LANES * (k + 1))
        ref[2 * j + k, :, 0:LANES] = real[:, cols]
        ref[2 * j + k, :, LANES:BLOCK] = imag[:, cols]


def get_tiles(ref, j):
    real = jnp.concatenate([ref[2 * j, :, 0:LANES], ref[2 * j + 1, :, 0:LANES]], axis=1)
    imag = jnp.concatenate([ref[2 * j, :, LANES:BLOCK], ref[2 * j + 1, :, LANES:BLOCK]], axis=1)
    return jnp.concatenate([real, imag], axis=0)


def box_columns(high_ref, low_ref, band, start, n):
    rows = n * high_ref.shape[1]

    def part(ref, d):
        lanes = band[2 * BLOCK * d : 2 * BLOCK * d + BLOCK]
        return jnp.dot(ref[start + d : start + d + n].reshape(rows, BLOCK), lanes, preferred_element_type=F32)

    return (part(high_ref, 0) + part(low_ref, 0)) + (part(high_ref, 1) + part(low_ref, 1))


def staggered(count, group, stages):
    starts = list(range(0, count, group))
    for t in range(len(starts) + len(stages) - 1):
        for s in reversed(range(len(stages))):
            if 0 <= t - s < len(starts):
                stages[s](starts[t - s])


def own_part(slc, second, core, turn, band, right):
    count = second.shape[0]
    group = OWN_GROUP

    def kernel(core_ref, a_ref, b_ref, w_ref, r_ref, y_ref, edge_ref, coh_ref, mark_ref, *scratch):
        mark_ref[...] = jnp.zeros(mark_ref.shape, F32)

        @pl.when(core_ref[0] == turn)
        def _():
            work(a_ref, b_ref, w_ref, r_ref, y_ref, edge_ref, coh_ref, *scratch)

    def work(a_ref, b_ref, w_ref, r_ref, y_ref, edge_ref, coh_ref, rows_ref, high_ref, low_ref, gh_ref, gl_ref):
        zero8 = jnp.zeros((8, LANES), F32)
        for slot in range(8):
            rows_ref[slot, 0:8] = zero8
            rows_ref[slot, 40:48] = zero8
        zero = jnp.zeros((128, LANES), BF16)
        for ref in (high_ref, low_ref):
            ref[0, :, 0:LANES] = zero
            ref[count, :, LANES:BLOCK] = zero
        sub = lax.broadcasted_iota(jnp.int32, (8, BLOCK), 0)
        row = lax.broadcasted_iota(jnp.int32, (32, BLOCK), 0)
        inner = (row >= 2) & (row < 30)

        def row_sums(g):
            for t in range(2 * g + 1 if g else 0, min(2 * (g + group) + 1, 2 * count)):
                j, k = t // 2, t % 2
                cols = slice(LANES * t, LANES * (t + 1))
                a0, a1 = a_ref[0, 0, :, cols], a_ref[0, 1, :, cols]
                b0, b1 = b_ref[j, 64 * k : 64 * k + 32], b_ref[j, 64 * k + 32 : 64 * k + 64]
                fields = (a0 * b0 + a1 * b1, a1 * b0 - a0 * b1, a0 * a0 + a1 * a1, b0 * b0 + b1 * b1)
                at, side = (t + 1) // 2, (t + 1) % 2
                lanes = slice(LANES * side, LANES * (side + 1))
                for f, field in enumerate(fields):
                    slot = 4 * (t % 2) + f
                    rows_ref[slot, 8:40] = field
                    total = field
                    for shift in (6, 7, 9, 10):
                        total = total + rows_ref[slot, shift : shift + 32]
                    high, low = split(total)
                    high_ref[at, 32 * f : 32 * f + 32, lanes] = high
                    low_ref[at, 32 * f : 32 * f + 32, lanes] = low

        def gamma(g):
            sums = box_columns(high_ref, low_ref, w_ref[...], g, group)
            for j in range(g, g + group):
                total = [sums[128 * (j - g) + 32 * f : 128 * (j - g) + 32 * f + 32] for f in range(4)]
                for f in range(4):
                    edge_ref[j, 8 * f : 8 * f + 8] = jnp.where(sub < 4, total[f][0:8], total[f][24:32])
                gr, gi, coherence = gamma_of(total)
                coh_ref[:, BLOCK * j : BLOCK * (j + 1)] = coherence
                gr, gi = jnp.where(inner, gr, 0.0), jnp.where(inner, gi, 0.0)
                rh, rl = split(gr)
                ih, il = split(gi)
                put_tiles(gh_ref, j, rh, ih)
                put_tiles(gl_ref, j, rl, il)

        def transform(g):
            m, n = 2 * g, 2 * group
            h, l = (ref[m : m + n].reshape(32 * n, BLOCK) for ref in (gh_ref, gl_ref))
            y = jnp.dot(jnp.concatenate([h, l, h], axis=1), r_ref[...], preferred_element_type=F32)
            y_ref[m : m + n] = y.reshape(n, 32, BLOCK)

        staggered(count, group, (row_sums, gamma, transform))

    return pl.pallas_call(
        kernel,
        out_shape=(
            jax.ShapeDtypeStruct((2 * count, 32, BLOCK), F32),
            jax.ShapeDtypeStruct((count, 32, BLOCK), F32),
            jax.ShapeDtypeStruct((32, BLOCK * count), F32),
            jax.ShapeDtypeStruct((8, LANES), F32),
        ),
        in_specs=[SMEM] + [VMEM] * 4,
        out_specs=(VMEM, VMEM, VMEM, VMEM),
        scratch_shapes=[
            pltpu.VMEM((8, 48, LANES), F32),
            pltpu.VMEM((count + 1, 128, BLOCK), BF16),
            pltpu.VMEM((count + 1, 128, BLOCK), BF16),
            pltpu.VMEM((2 * count, 32, BLOCK), BF16),
            pltpu.VMEM((2 * count, 32, BLOCK), BF16),
        ],
        compiler_params=PARAMS,
        cost_estimate=cost(4 << 30, 12 << 20),
        name="own_part",
    )(core, slc, second, band, right)


def with_edges(late, early, halos, core, right, right_inv, left, left_inv, band, mean):
    count = late[1].shape[0]
    group = EDGE_GROUP

    def kernel(core_ref, *refs):
        @pl.when(core_ref[0] == 0)
        def _():
            work(True, *refs[0:3], *refs[6:])

        @pl.when(core_ref[0] != 0)
        def _():
            work(False, *refs[3:])

    def work(even, yin_ref, edge_ref, coh_ref, near_ref, away_ref,
             r_ref, ri_ref, l_ref, li_ref, w_ref, m_ref, o_ref,
             part_ref, high_ref, low_ref, g_ref, y_ref, z_ref, vh_ref, vl_ref, strip_ref, out_ref, sem):
        copies = [pltpu.make_async_copy(coh_ref.at[8:24], o_ref.at[0, 0, 8:24], sem.at[0])]
        copies[0].start()
        odd_row = lax.broadcasted_iota(jnp.int32, (8, LANES), 0) % 2 == 1
        sub = lax.broadcasted_iota(jnp.int32, (8, BLOCK), 0)
        outer = (sub < 2) | (sub >= 6)
        part_ref[...] = jnp.zeros(part_ref.shape, F32)
        for j in range(count):
            for place in range(2):
                a, b = (
                    near_ref[i, j] if even == (place == 1) else away_ref[i, j]
                    for i in range(2)
                )
                mixed = a * pltpu.roll(b, 4, 0)
                same, aa, bb = a * b, a * a, b * b
                fields = (
                    same + pltpu.roll(same, 4, 0),
                    pltpu.roll(mixed, 4, 0) - mixed,
                    aa + pltpu.roll(aa, 4, 0),
                    bb + pltpu.roll(bb, 4, 0),
                )
                for f, field in enumerate(fields):
                    if place == 0:
                        field = jnp.where(odd_row, field, field + pltpu.roll(field, 7, 0))
                    else:
                        field = jnp.where(odd_row, field + pltpu.roll(field, 1, 0), field)
                    row = 8 * f + 6 * place
                    part_ref[j, row : row + 2, LANES:BLOCK] = field[0:2]
                    part_ref[j + 1, row : row + 2, 0:LANES] = field[2:4]
        for j in range(count + 1):
            high_ref[j], low_ref[j] = split(part_ref[j])

        def gamma(g):
            more = box_columns(high_ref, low_ref, w_ref[...], g, group)
            for j in range(g, g + group):
                at = 32 * (j - g)
                total = [edge_ref[j, 8 * f : 8 * f + 8] + more[at + 8 * f : at + 8 * f + 8] for f in range(4)]
                gr, gi, coherence = gamma_of(total)
                cols = slice(BLOCK * j, BLOCK * (j + 1))
                strip_ref[0, :, cols] = jnp.where(sub < 2, coherence, coh_ref[0:8, cols])
                strip_ref[1, :, cols] = jnp.where(sub >= 6, coherence, coh_ref[24:32, cols])
                put_tiles(g_ref, j, jnp.where(outer, gr, 0.0), jnp.where(outer, gi, 0.0))

        def transform(g):
            m, n = 2 * g, 2 * group
            h, l = split(g_ref[m : m + n].reshape(8 * n, BLOCK))
            y = jnp.dot(jnp.concatenate([h, l, h], axis=1), r_ref[...], preferred_element_type=F32)
            for t in range(n):
                more = y[8 * t : 8 * t + 8]
                y_ref[m + t, 0:8] = yin_ref[m + t, 0:8] + jnp.where(sub < 4, more, 0.0)
                y_ref[m + t, 8:24] = yin_ref[m + t, 8:24]
                y_ref[m + t, 24:32] = yin_ref[m + t, 24:32] + jnp.where(sub < 4, 0.0, more)

        def forward(g):
            for j in range(g, g + group):
                h, l = split(get_tiles(y_ref, j))
                z_ref[j] = jnp.dot(l_ref[...], jnp.concatenate([h, l, h], axis=0), preferred_element_type=F32)

        sums = {}

        def backward(g):
            parts = []
            for j in range(g, g + group):
                zr, zi = z_ref[j, 0:32], z_ref[j, 32:64]
                weight = lax.rsqrt(lax.rsqrt(zr * zr + zi * zi + 1e-06))
                parts.append(weight[0:8] + weight[8:16] + weight[16:24] + weight[24:32])
                h, l = split(jnp.concatenate([zr * weight, zi * weight], axis=0))
                v = jnp.dot(li_ref[...], jnp.concatenate([h, l, h], axis=0), preferred_element_type=F32)
                h, l = split(v)
                put_tiles(vh_ref, j, h[0:32], h[32:64])
                put_tiles(vl_ref, j, l[0:32], l[32:64])
            h, l = split(jnp.concatenate(parts, axis=0))
            total = jnp.dot(jnp.concatenate([h, l], axis=1), m_ref[...], preferred_element_type=F32)
            sums[g] = 1.0 / jnp.sum(total.reshape(group, 8, BLOCK), axis=1, keepdims=True)

        def finish(g):
            m, n = 2 * g, 2 * group
            h, l = (ref[m : m + n].reshape(32 * n, BLOCK) for ref in (vh_ref, vl_ref))
            out = jnp.dot(jnp.concatenate([h, l, h], axis=1), ri_ref[...], preferred_element_type=F32)
            for t in range(n):
                factor = sums[g][t // 2, :, LANES * (t % 2) : LANES * (t % 2 + 1)]
                cols = slice(LANES * (m + t), LANES * (m + t + 1))
                out_ref[0, :, cols] = out[32 * t : 32 * t + 32, 0:LANES] * factor
                out_ref[1, :, cols] = out[32 * t : 32 * t + 32, LANES:BLOCK] * factor
                if (t + 1) % OUT_TILES == 0:
                    cols = slice(LANES * (m + t + 1 - OUT_TILES), LANES * (m + t + 1))
                    at = sem.at[3 + (m + t) // OUT_TILES]
                    copy = pltpu.make_async_copy(out_ref.at[:, :, cols], o_ref.at[0, 1:3, :, cols], at)
                    copy.start()
                    copies.append(copy)
            if g + group == count:
                for i in range(2):
                    copy = pltpu.make_async_copy(strip_ref.at[i], o_ref.at[0, 0, 24 * i : 24 * i + 8], sem.at[1 + i])
                    copy.start()
                    copies.append(copy)

        staggered(count, group, (gamma, transform, forward, backward, finish))
        for copy in copies:
            copy.wait()

    return pl.pallas_call(
        kernel,
        out_shape=jax.ShapeDtypeStruct((1, 3, 32, BLOCK * count), F32),
        in_specs=[SMEM] + [VMEM] * 14,
        out_specs=pl.BlockSpec(memory_space=pltpu.HBM),
        scratch_shapes=[
            pltpu.VMEM((count + 1, 32, BLOCK), F32),
            pltpu.VMEM((count + 1, 32, BLOCK), BF16),
            pltpu.VMEM((count + 1, 32, BLOCK), BF16),
            pltpu.VMEM((2 * count, 8, BLOCK), F32),
            pltpu.VMEM((2 * count, 32, BLOCK), F32),
            pltpu.VMEM((count, 64, BLOCK), F32),
            pltpu.VMEM((2 * count, 32, BLOCK), BF16),
            pltpu.VMEM((2 * count, 32, BLOCK), BF16),
            pltpu.VMEM((2, 8, BLOCK * count), F32),
            pltpu.VMEM((2, 32, BLOCK * count), F32),
            pltpu.SemaphoreType.DMA((3 + 2 * count // OUT_TILES,)),
        ],
        compiler_params=PARAMS,
        cost_estimate=cost(8 << 30, 8 << 20),
        name="with_edges",
    )(core, *late, *early, *halos, right, right_inv, left, left_inv, band, mean)


def on_device(slc, pair_index):
    right, right_inv, left, left_inv, band, mean = (jnp.asarray(m) for m in constants())
    blocks = lax.axis_size("rows")
    core = (lax.axis_index("rows") % 2).astype(jnp.int32).reshape(1)
    between = range(1, blocks - 1, 2)
    far = [(i, i + 1) for i in between] + [(i + 1, i) for i in between]
    pairs = [(i, i ^ 1) for i in range(blocks)]

    held = lax.all_to_all(spread_chunks(slc, pair_index, core), "acq", 0, 0)
    second = lax.all_to_all(pick_chunks(held), "acq", 0, 0)
    *early, mark = own_part(slc, second, core, 1, band, right)
    away = lax.ppermute(edge_rows(slc, second, core, mark, False), "rows", far)
    *late, mark = own_part(slc, second, core, 0, band, right)
    near = lax.ppermute(edge_rows(slc, second, core, mark, True), "rows", pairs)
    return with_edges(
        late, early, (near, away), core, right, right_inv, left, left_inv, band, mean,
    )


def solution(mesh):
    return jax.shard_map(
        on_device,
        mesh=mesh,
        in_specs=(P("acq", None, "rows", None), P("acq", None)),
        out_specs=P("acq", None, "rows", None),
        check_vma=False,
    )
```

```python
import functools

import jax
import jax.numpy as jnp
import ml_dtypes
import numpy as np
from jax import lax
from jax.experimental import pallas as pl
from jax.experimental.pallas import tpu as pltpu
from jax.sharding import PartitionSpec as P

LOOK_R = 5
LOOK_C = 19
PATCH = 32
LANES = 128
BLOCK = 256
OWN_GROUP = 16
LATE_GROUPS = 3
EARLY_GROUPS = 4
EDGE_GROUPS = {0: 10, 10: 6}
OUT_TILES = 2
VMEM = pl.BlockSpec(memory_space=pltpu.VMEM)
SMEM = pl.BlockSpec(memory_space=pltpu.SMEM)
PARAMS = pltpu.CompilerParams(vmem_limit_bytes=40 * 1024 * 1024)
F32 = jnp.float32
BF16 = jnp.bfloat16


def cost(flops, moved):
    return pl.CostEstimate(flops=flops, bytes_accessed=moved, transcendentals=0)


def halves(matrix):
    high = matrix.astype(ml_dtypes.bfloat16)
    low = (matrix - high.astype(np.float64)).astype(ml_dtypes.bfloat16)
    return high, low


def split(x):
    high = x.astype(BF16)
    low = (x - high.astype(F32)).astype(BF16)
    return high, low


def constants():
    index = np.arange(PATCH)
    phase = 2.0 * np.pi / PATCH * (index[:, None] * index[None, :] % PATCH)
    c, s = np.cos(phase), np.sin(phase)
    eye = np.eye(LANES // PATCH)
    cb, sb = np.kron(eye, c), np.kron(eye, s)

    def three_rows(m):
        h, l = halves(m)
        return np.concatenate([h, h, l], axis=0)

    def three_cols(m):
        h, l = halves(m)
        return np.concatenate([h, h, l], axis=1)

    right = three_rows(np.block([[cb, -sb], [sb, cb]]))
    right_inv = three_rows(np.block([[cb, sb], [-sb, cb]]) / (PATCH * PATCH))
    left = three_cols(np.block([[c, s], [-s, c]]))
    left_inv = three_cols(np.block([[c, -s], [s, c]]))
    half = LOOK_C // 2
    row, col = np.arange(BLOCK)[:, None], np.arange(BLOCK)[None, :]
    near = (np.abs(row - LANES - col) <= half).astype(ml_dtypes.bfloat16)
    far = (np.abs(row + LANES - col) <= half).astype(ml_dtypes.bfloat16)
    band = np.concatenate([near, near, far, far], axis=0)
    mean = np.kron(np.eye(BLOCK // PATCH), np.full((PATCH, PATCH), 1.0 / (PATCH * PATCH))).astype(ml_dtypes.bfloat16)
    mean = np.concatenate([mean, mean], axis=0)
    return right, right_inv, left, left_inv, band, mean


def spread_chunks(slc, pair_index, core):
    count = slc.shape[3] // BLOCK

    def kernel(core_ref, x_ref, pair_ref, o_ref, wanted_ref, held_ref, pair_sem, in_sem, out_sem):
        pair_copy = pltpu.make_async_copy(pair_ref, wanted_ref, pair_sem)
        pair_copy.start()

        def start(first, last, sem):
            for j in range(first, last):
                for k in range(2):
                    cols = slice(BLOCK * j + LANES * k, BLOCK * j + LANES * (k + 1))
                    for c in range(2):
                        rows = slice(64 * k + 32 * c, 64 * k + 32 * c + 32)
                        pltpu.make_async_copy(x_ref.at[0, c, :, cols], held_ref.at[j, rows], sem).start()

        def wait(first, last, sem):
            part = held_ref.at[first:last, 0:128]
            pltpu.make_async_copy(part, part, sem).wait()

        def out(first, last, sem):
            return pltpu.make_async_copy(held_ref.at[first:last], o_ref.at[first:last], sem)

        def fill():
            pair_copy.wait()
            wanted = jnp.full((8, LANES), wanted_ref[0, 1].astype(F32))
            for j in range(count):
                held_ref[j, 128:136] = wanted

        @pl.when(core_ref[0] == 0)
        def _():
            ends = [count * (g + 1) // LATE_GROUPS for g in range(LATE_GROUPS)]
            for g, (first, last) in enumerate(zip([0] + ends, ends)):
                start(first, last, in_sem.at[g])
                if g == 0:
                    fill()
                wait(first, last, in_sem.at[g])
                copy = out(first, last, out_sem.at[g])
                copy.start()
                copy.wait()

        @pl.when(core_ref[0] != 0)
        def _():
            n = count // EARLY_GROUPS
            copies = []

            def send(groups, rows, sem):
                copy = pltpu.make_async_copy(held_ref.at[groups, rows], o_ref.at[groups, rows], sem)
                copy.start()
                copies.append(copy)

            for g in range(EARLY_GROUPS):
                start(g * n, g * n + n, in_sem.at[g])
            for g in range(EARLY_GROUPS):
                wait(g * n, g * n + n, in_sem.at[g])
                send(slice(g * n, g * n + n), slice(0, 128), out_sem.at[g])
            fill()
            send(slice(0, count), slice(128, 136), out_sem.at[EARLY_GROUPS])
            for copy in copies:
                copy.wait()

    hbm = pl.BlockSpec(memory_space=pltpu.HBM)
    return pl.pallas_call(
        kernel,
        out_shape=jax.ShapeDtypeStruct((count, 136, LANES), F32),
        in_specs=[SMEM, hbm, hbm],
        out_specs=hbm,
        scratch_shapes=[
            pltpu.SMEM((1, 2), jnp.int32),
            pltpu.VMEM((count, 136, LANES), F32),
            pltpu.SemaphoreType.DMA,
            pltpu.SemaphoreType.DMA((max(LATE_GROUPS, EARLY_GROUPS),)),
            pltpu.SemaphoreType.DMA((max(LATE_GROUPS, EARLY_GROUPS + 1),)),
        ],
        compiler_params=pltpu.CompilerParams(vmem_limit_bytes=60 * 1024 * 1024),
        cost_estimate=cost(0, 2 << 20),
        name="spread_chunks",
    )(core, slc, pair_index)


def pick_chunks(held):
    count = held.shape[0]

    def kernel(v_ref, o_ref):
        for p in range(count):
            wanted = v_ref[p, 128:129, 0:1][0, 0].astype(jnp.int32)
            o_ref[p] = v_ref[wanted, 0:128]

    return pl.pallas_call(
        kernel,
        out_shape=jax.ShapeDtypeStruct((count, 128, LANES), F32),
        in_specs=[VMEM],
        out_specs=VMEM,
        compiler_params=PARAMS,
        cost_estimate=cost(0, 2 << 20),
        name="pick_chunks",
    )(held)


def first_sides(core, top, low):
    return jnp.where(core == 0, low, top), jnp.where(core == 0, top, low)


def edge_rows(slc, second, core, mark, near):
    count = second.shape[0]

    def kernel(core_ref, a_ref, b_ref, mark_ref, o_ref):
        pick = 0 if near else 1
        for j in range(count):
            for k in range(2):
                cols = slice(BLOCK * j + LANES * k, BLOCK * j + LANES * (k + 1))
                for c in range(2):
                    at = slice(4 * c + 2 * k, 4 * c + 2 * k + 2)
                    base = 64 * k + 32 * c
                    o_ref[0, j, at] = first_sides(core_ref[0], a_ref[0, c, 0:2, cols], a_ref[0, c, 30:32, cols])[pick]
                    o_ref[1, j, at] = first_sides(core_ref[0], b_ref[j, base : base + 2], b_ref[j, base + 30 : base + 32])[pick]

    return pl.pallas_call(
        kernel,
        out_shape=jax.ShapeDtypeStruct((2, count, 8, LANES), F32),
        in_specs=[SMEM, VMEM, VMEM, VMEM],
        out_specs=VMEM,
        compiler_params=PARAMS,
        cost_estimate=cost(0, 1 << 20),
        name="edge_rows_near" if near else "edge_rows_away",
    )(core, slc, second, mark)


def gamma_of(total):
    scale = lax.rsqrt(total[2] * total[3] + 1e-06)
    gr, gi = total[0] * scale, total[1] * scale
    return gr, gi, jnp.sqrt(gr * gr + gi * gi)


def put_tiles(ref, j, real, imag):
    for k in range(2):
        cols = slice(LANES * k, LANES * (k + 1))
        ref[2 * j + k, :, 0:LANES] = real[:, cols]
        ref[2 * j + k, :, LANES:BLOCK] = imag[:, cols]


def get_tiles(ref, j):
    real = jnp.concatenate([ref[2 * j, :, 0:LANES], ref[2 * j + 1, :, 0:LANES]], axis=1)
    imag = jnp.concatenate([ref[2 * j, :, LANES:BLOCK], ref[2 * j + 1, :, LANES:BLOCK]], axis=1)
    return jnp.concatenate([real, imag], axis=0)


def box_columns(high_ref, low_ref, band, start, n):
    rows = n * high_ref.shape[1]
    parts = [ref[start + d : start + d + n].reshape(rows, BLOCK) for d in range(2) for ref in (high_ref, low_ref)]
    return jnp.dot(jnp.concatenate(parts, axis=1), band, preferred_element_type=F32)


def staggered(starts, stages):
    for t in range(len(starts) + len(stages) - 1):
        for s in reversed(range(len(stages))):
            if 0 <= t - s < len(starts):
                stages[s](starts[t - s])


def own_part(slc, second, core, turn, band, right):
    count = second.shape[0]
    group = OWN_GROUP

    def kernel(core_ref, a_ref, b_ref, w_ref, r_ref, y_ref, edge_ref, coh_ref, mark_ref, *scratch):
        mark_ref[...] = jnp.zeros(mark_ref.shape, F32)

        @pl.when(core_ref[0] == turn)
        def _():
            work(a_ref, b_ref, w_ref, r_ref, y_ref, edge_ref, coh_ref, *scratch)

    def work(a_ref, b_ref, w_ref, r_ref, y_ref, edge_ref, coh_ref, rows_ref, high_ref, low_ref, gh_ref, gl_ref):
        zero8 = jnp.zeros((8, LANES), F32)
        for slot in range(8):
            rows_ref[slot, 0:8] = zero8
            rows_ref[slot, 40:48] = zero8
        zero = jnp.zeros((128, LANES), BF16)
        for ref in (high_ref, low_ref):
            ref[0, :, 0:LANES] = zero
            ref[count, :, LANES:BLOCK] = zero
        sub = lax.broadcasted_iota(jnp.int32, (8, BLOCK), 0)
        row = lax.broadcasted_iota(jnp.int32, (32, BLOCK), 0)
        inner = (row >= 2) & (row < 30)

        def row_sums(g):
            for t in range(2 * g + 1 if g else 0, min(2 * (g + group) + 1, 2 * count)):
                j, k = t // 2, t % 2
                cols = slice(LANES * t, LANES * (t + 1))
                a0, a1 = a_ref[0, 0, :, cols], a_ref[0, 1, :, cols]
                b0, b1 = b_ref[j, 64 * k : 64 * k + 32], b_ref[j, 64 * k + 32 : 64 * k + 64]
                fields = (a0 * b0 + a1 * b1, a1 * b0 - a0 * b1, a0 * a0 + a1 * a1, b0 * b0 + b1 * b1)
                at, side = (t + 1) // 2, (t + 1) % 2
                lanes = slice(LANES * side, LANES * (side + 1))
                for f, field in enumerate(fields):
                    slot = 4 * (t % 2) + f
                    rows_ref[slot, 8:40] = field
                    total = field
                    for shift in (6, 7, 9, 10):
                        total = total + rows_ref[slot, shift : shift + 32]
                    high, low = split(total)
                    high_ref[at, 32 * f : 32 * f + 32, lanes] = high
                    low_ref[at, 32 * f : 32 * f + 32, lanes] = low

        def gamma(g):
            sums = box_columns(high_ref, low_ref, w_ref[...], g, group)
            for j in range(g, g + group):
                total = [sums[128 * (j - g) + 32 * f : 128 * (j - g) + 32 * f + 32] for f in range(4)]
                for f in range(4):
                    edge_ref[j, 8 * f : 8 * f + 8] = jnp.where(sub < 4, total[f][0:8], total[f][24:32])
                gr, gi, coherence = gamma_of(total)
                coh_ref[:, BLOCK * j : BLOCK * (j + 1)] = coherence
                gr, gi = jnp.where(inner, gr, 0.0), jnp.where(inner, gi, 0.0)
                rh, rl = split(gr)
                ih, il = split(gi)
                put_tiles(gh_ref, j, rh, ih)
                put_tiles(gl_ref, j, rl, il)

        def transform(g):
            m, n = 2 * g, 2 * group
            h, l = (ref[m : m + n].reshape(32 * n, BLOCK) for ref in (gh_ref, gl_ref))
            y = jnp.dot(jnp.concatenate([h, l, h], axis=1), r_ref[...], preferred_element_type=F32)
            y_ref[m : m + n] = y.reshape(n, 32, BLOCK)

        staggered(list(range(0, count, group)), (row_sums, gamma, transform))

    return pl.pallas_call(
        kernel,
        out_shape=(
            jax.ShapeDtypeStruct((2 * count, 32, BLOCK), F32),
            jax.ShapeDtypeStruct((count, 32, BLOCK), F32),
            jax.ShapeDtypeStruct((32, BLOCK * count), F32),
            jax.ShapeDtypeStruct((8, LANES), F32),
        ),
        in_specs=[SMEM] + [VMEM] * 4,
        out_specs=(VMEM, VMEM, VMEM, VMEM),
        scratch_shapes=[
            pltpu.VMEM((8, 48, LANES), F32),
            pltpu.VMEM((count + 1, 128, BLOCK), BF16),
            pltpu.VMEM((count + 1, 128, BLOCK), BF16),
            pltpu.VMEM((2 * count, 32, BLOCK), BF16),
            pltpu.VMEM((2 * count, 32, BLOCK), BF16),
        ],
        compiler_params=PARAMS,
        cost_estimate=cost(4 << 30, 12 << 20),
        name="own_part",
    )(core, slc, second, band, right)


def with_edges(late, early, halos, core, right, right_inv, left, left_inv, band, mean):
    count = late[1].shape[0]

    def kernel(core_ref, *refs):
        @pl.when(core_ref[0] == 0)
        def _():
            work(True, *refs[0:3], *refs[6:])

        @pl.when(core_ref[0] != 0)
        def _():
            work(False, *refs[3:])

    def work(even, yin_ref, edge_ref, coh_ref, near_ref, away_ref,
             r_ref, ri_ref, l_ref, li_ref, w_ref, m_ref, o_ref,
             part_ref, high_ref, low_ref, g_ref, y_ref, z_ref, vh_ref, vl_ref, strip_ref, out_ref, sem):
        copies = [pltpu.make_async_copy(coh_ref.at[8:24], o_ref.at[0, 0, 8:24], sem.at[0])]
        copies[0].start()
        odd_row = lax.broadcasted_iota(jnp.int32, (8, LANES), 0) % 2 == 1
        sub = lax.broadcasted_iota(jnp.int32, (8, BLOCK), 0)
        outer = (sub < 2) | (sub >= 6)
        part_ref[...] = jnp.zeros(part_ref.shape, F32)
        for j in range(count):
            for place in range(2):
                a, b = (
                    near_ref[i, j] if even == (place == 1) else away_ref[i, j]
                    for i in range(2)
                )
                mixed = a * pltpu.roll(b, 4, 0)
                same, aa, bb = a * b, a * a, b * b
                fields = (
                    same + pltpu.roll(same, 4, 0),
                    pltpu.roll(mixed, 4, 0) - mixed,
                    aa + pltpu.roll(aa, 4, 0),
                    bb + pltpu.roll(bb, 4, 0),
                )
                for f, field in enumerate(fields):
                    if place == 0:
                        field = jnp.where(odd_row, field, field + pltpu.roll(field, 7, 0))
                    else:
                        field = jnp.where(odd_row, field + pltpu.roll(field, 1, 0), field)
                    row = 8 * f + 6 * place
                    part_ref[j, row : row + 2, LANES:BLOCK] = field[0:2]
                    part_ref[j + 1, row : row + 2, 0:LANES] = field[2:4]
        for j in range(count + 1):
            high_ref[j], low_ref[j] = split(part_ref[j])

        def gamma(g):
            group = EDGE_GROUPS[g]
            more = box_columns(high_ref, low_ref, w_ref[...], g, group)
            for j in range(g, g + group):
                at = 32 * (j - g)
                total = [edge_ref[j, 8 * f : 8 * f + 8] + more[at + 8 * f : at + 8 * f + 8] for f in range(4)]
                gr, gi, coherence = gamma_of(total)
                cols = slice(BLOCK * j, BLOCK * (j + 1))
                strip_ref[0, :, cols] = jnp.where(sub < 2, coherence, coh_ref[0:8, cols])
                strip_ref[1, :, cols] = jnp.where(sub >= 6, coherence, coh_ref[24:32, cols])
                put_tiles(g_ref, j, jnp.where(outer, gr, 0.0), jnp.where(outer, gi, 0.0))

        def transform(g):
            group = EDGE_GROUPS[g]
            if g + group == count:
                strips()
            m, n = 2 * g, 2 * group
            h, l = split(g_ref[m : m + n].reshape(8 * n, BLOCK))
            y = jnp.dot(jnp.concatenate([h, l, h], axis=1), r_ref[...], preferred_element_type=F32)
            for t in range(n):
                more = y[8 * t : 8 * t + 8]
                y_ref[m + t, 0:8] = yin_ref[m + t, 0:8] + jnp.where(sub < 4, more, 0.0)
                y_ref[m + t, 8:24] = yin_ref[m + t, 8:24]
                y_ref[m + t, 24:32] = yin_ref[m + t, 24:32] + jnp.where(sub < 4, 0.0, more)

        def strips():
            for i in range(2):
                copy = pltpu.make_async_copy(strip_ref.at[i], o_ref.at[0, 0, 24 * i : 24 * i + 8], sem.at[1 + i])
                copy.start()
                copies.append(copy)

        def forward(g):
            group = EDGE_GROUPS[g]
            for j in range(g, g + group):
                h, l = split(get_tiles(y_ref, j))
                z_ref[j] = jnp.dot(l_ref[...], jnp.concatenate([h, l, h], axis=0), preferred_element_type=F32)

        sums = {}

        def backward(g):
            group = EDGE_GROUPS[g]
            parts = []
            for j in range(g, g + group):
                zr, zi = z_ref[j, 0:32], z_ref[j, 32:64]
                weight = lax.rsqrt(lax.rsqrt(zr * zr + zi * zi + 1e-06))
                parts.append(weight[0:8] + weight[8:16] + weight[16:24] + weight[24:32])
                h, l = split(jnp.concatenate([zr * weight, zi * weight], axis=0))
                v = jnp.dot(li_ref[...], jnp.concatenate([h, l, h], axis=0), preferred_element_type=F32)
                h, l = split(v)
                put_tiles(vh_ref, j, h[0:32], h[32:64])
                put_tiles(vl_ref, j, l[0:32], l[32:64])
            h, l = split(jnp.concatenate(parts, axis=0))
            total = jnp.dot(jnp.concatenate([h, l], axis=1), m_ref[...], preferred_element_type=F32)
            sums[g] = 1.0 / jnp.sum(total.reshape(group, 8, BLOCK), axis=1, keepdims=True)

        def finish(g):
            group = EDGE_GROUPS[g]
            m, n = 2 * g, 2 * group
            h, l = (ref[m : m + n].reshape(32 * n, BLOCK) for ref in (vh_ref, vl_ref))
            out = jnp.dot(jnp.concatenate([h, l, h], axis=1), ri_ref[...], preferred_element_type=F32)
            for t in range(n):
                factor = sums[g][t // 2, :, LANES * (t % 2) : LANES * (t % 2 + 1)]
                cols = slice(LANES * (m + t), LANES * (m + t + 1))
                out_ref[0, :, cols] = out[32 * t : 32 * t + 32, 0:LANES] * factor
                out_ref[1, :, cols] = out[32 * t : 32 * t + 32, LANES:BLOCK] * factor
                if (t + 1) % OUT_TILES == 0:
                    cols = slice(LANES * (m + t + 1 - OUT_TILES), LANES * (m + t + 1))
                    at = sem.at[3 + (m + t) // OUT_TILES]
                    copy = pltpu.make_async_copy(out_ref.at[:, :, cols], o_ref.at[0, 1:3, :, cols], at)
                    copy.start()
                    copies.append(copy)

        staggered(list(EDGE_GROUPS), (gamma, transform, forward, backward, finish))
        for copy in copies:
            copy.wait()

    return pl.pallas_call(
        kernel,
        out_shape=jax.ShapeDtypeStruct((1, 3, 32, BLOCK * count), F32),
        in_specs=[SMEM] + [VMEM] * 14,
        out_specs=pl.BlockSpec(memory_space=pltpu.HBM),
        scratch_shapes=[
            pltpu.VMEM((count + 1, 32, BLOCK), F32),
            pltpu.VMEM((count + 1, 32, BLOCK), BF16),
            pltpu.VMEM((count + 1, 32, BLOCK), BF16),
            pltpu.VMEM((2 * count, 8, BLOCK), F32),
            pltpu.VMEM((2 * count, 32, BLOCK), F32),
            pltpu.VMEM((count, 64, BLOCK), F32),
            pltpu.VMEM((2 * count, 32, BLOCK), BF16),
            pltpu.VMEM((2 * count, 32, BLOCK), BF16),
            pltpu.VMEM((2, 8, BLOCK * count), F32),
            pltpu.VMEM((2, 32, BLOCK * count), F32),
            pltpu.SemaphoreType.DMA((3 + 2 * count // OUT_TILES,)),
        ],
        compiler_params=PARAMS,
        cost_estimate=cost(8 << 30, 8 << 20),
        name="with_edges",
    )(core, *late, *early, *halos, right, right_inv, left, left_inv, band, mean)


def on_device(slc, pair_index):
    right, right_inv, left, left_inv, band, mean = (jnp.asarray(m) for m in constants())
    blocks = lax.axis_size("rows")
    core = (lax.axis_index("rows") % 2).astype(jnp.int32).reshape(1)
    between = range(1, blocks - 1, 2)
    far = [(i, i + 1) for i in between] + [(i + 1, i) for i in between]
    pairs = [(i, i ^ 1) for i in range(blocks)]

    held = lax.all_to_all(spread_chunks(slc, pair_index, core), "acq", 0, 0)
    second = lax.all_to_all(pick_chunks(held), "acq", 0, 0)
    *early, mark = own_part(slc, second, core, 1, band, right)
    away = lax.ppermute(edge_rows(slc, second, core, mark, False), "rows", far)
    *late, mark = own_part(slc, second, core, 0, band, right)
    near = lax.ppermute(edge_rows(slc, second, core, mark, True), "rows", pairs)
    return with_edges(
        late, early, (near, away), core, right, right_inv, left, left_inv, band, mean,
    )


def solution(mesh):
    return jax.shard_map(
        on_device,
        mesh=mesh,
        in_specs=(P("acq", None, "rows", None), P("acq", None)),
        out_specs=P("acq", None, "rows", None),
        check_vma=False,
    )
```
